512 devices in a mesh: blk: 128 (over x, z, y_hi, core), feat: 4 (over y_lo).
Axes of the slice: x: 4, y: 8 (y_hi: 2, y_lo: 4; y = y_hi * 4 + y_lo), z: 8, core: 2. Of those that a mesh axis runs over, the one named last changes fastest.
Arguments:
- features: bfloat16 [256, 32768], P('feat', 'blk'), may hold values from -6 to 6
- near_tiles: bfloat16 [32768, 7, 256], P('blk'), may hold values from 0 to 1
- far_tiles: bfloat16 [12288, 128, 128], P('blk'), may hold values from 0 to 1
- far_source: int32 [12288, 1], P('blk'), may hold values from 0 to 127; in each aligned block of 96 rows (0 to 95, 96 to 191, ...) at most 2 rows name the same one
- far_index: int32 [12288, 2], P('blk'), may hold values from 0 to 1
- weight: bfloat16 [256, 256], P(None, 'feat'), may hold values from -0.375 to 0.375
- bias: float32 [256], P('feat'), may hold values from -3 to 3
- grad_out: bfloat16 [256, 32768], P('feat', 'blk'), may hold values from -6 to 6
Outputs:
- activated: bfloat16 [256, 32768], P('feat', 'blk')
- grad_feat: bfloat16 [256, 32768], P('feat', 'blk')
- grad_weight: float32 [256, 256], P(None, 'feat')
- grad_bias: float32 [256], P('feat')
The draws below stay inside these ranges and needn't reach their ends.
Inputs may be any that keep to these rules, and one draw needn't show every extreme that they name: `far_source`: in the 96 rows of one row block no value appears more than 2 times, and some value appears exactly 2 times.
All inputs are finite; a program needn't handle non-finite values.
Results may differ from the reference program's by a relative error of at most 0.01.
Values may be sent and summed in bfloat16 or wider, within the bound.
A program may use at most 64 MiB of HBM per device.

```python
import math
import jax
import jax.numpy as jnp
import numpy as np
from jax import lax

H = 256
ROWS = 256
TILE = 128
MOST = 2
TPD = 2
FAR = 96
NODES = 32768
FAR_ALL = 12288
N_BLK = 128


def adjacency_values(key, shape):
    count = 7 * ROWS + FAR * TILE // TPD
    base_scale = 3.0 / math.sqrt(count)
    subkeys = jax.random.split(key, 2)
    magnitude = jax.random.uniform(subkeys[0], shape, jnp.float32)
    present = jax.random.uniform(subkeys[1], shape, jnp.float32) < 0.6
    values = jnp.where(present, magnitude, 0.0) * base_scale
    values = jnp.minimum(values, 1.0)
    return values.astype(jnp.bfloat16)


def draw_near_tiles(key, part):
    return adjacency_values(jax.random.fold_in(key, 11), (NODES, 7, ROWS))


def draw_far_tiles(key, part):
    return adjacency_values(jax.random.fold_in(key, 23), (FAR_ALL, TILE, TILE))


def touch_ends(array, own_key, smallest, top_value):
    longest = array.shape.index(max(array.shape))
    spots = []
    for shift in (0, 1):
        where = [jax.random.randint(jax.random.fold_in(own_key, axis), (), 0, length) for axis, length in enumerate(array.shape)]
        where[longest] = (where[longest] + shift) % array.shape[longest]
        spots.append(tuple(where))
    return array.at[spots[0]].set(smallest).at[spots[1]].set(top_value)


def level_of(own_key, dims, shards, smallest, top_value):
    loudness = 1.0
    for position, shards_of in shards:
        steps = jax.random.uniform(jax.random.fold_in(jax.random.fold_in(own_key, 6), position), (shards_of,), jnp.float32, smallest / len(shards), top_value / len(shards))
        loudness = loudness * jnp.repeat(jnp.exp(steps), dims[position] // shards_of).reshape((-1,) + (1,) * (len(dims) - 1 - position))
    return loudness


def assign_block(stream_key, own, number, rows, number_of, top, most, skew):
    sequence = jax.random.permutation(stream_key, number_of)
    packed, common = load_shares(number_of, rows * top, most, skew, True), load_shares(number_of, rows * top, most, skew, False)
    places = jnp.arange(number_of)

    def named(sizes, offset_by):
        used = int((sizes > 0).sum())
        fixed = max(1, used // 4)
        shifted = fixed + (places - fixed + offset_by * (used - fixed)) % max(1, number_of - fixed)
        return jnp.zeros((number_of,), jnp.int32).at[sequence[jnp.where(places < fixed, places, shifted)]].set(jnp.asarray(sizes, jnp.int32))

    sizes = jnp.where(number % 4 == 0, named(packed, number // 4), named(common, number - number // 4 - 1))
    mixed = jax.random.permutation(jax.random.fold_in(own, 3), number_of)
    donor, receiver = mixed[0:number_of // 2 * 2:2], mixed[1:number_of // 2 * 2:2]
    margin = jnp.minimum(sizes[donor] - 1, most - sizes[receiver]) // 2
    margin = jnp.where((donor == sequence[0]) | (receiver == sequence[0]) | (sizes[receiver] == 0), 0, jnp.maximum(margin, 0))
    shifted = jax.random.randint(jax.random.fold_in(own, 4), (number_of // 2,), 0, 1 << 20) % (margin + 1)
    sizes = sizes.at[donor].add(-shifted).at[receiver].add(shifted)
    members = jnp.searchsorted(jnp.cumsum(sizes), jnp.arange(rows * top), side="right").astype(jnp.int32)
    table = members.reshape(top, rows).T
    table = table[jax.random.permutation(jax.random.fold_in(own, 1), rows)]
    offset_by = jax.random.randint(jax.random.fold_in(own, 2), (rows, 1), 0, top)
    return jnp.take_along_axis(table, (jnp.arange(top)[None, :] + offset_by) % top, axis=1)


def load_shares(amount, total, reach, slope, full):
    portions = [(1 << 20) // math.isqrt(rank ** slope) + 1 for rank in range(1, amount + 1)]
    largest = reach if full else min(reach, max(-(-total // amount), total * portions[0] // sum(portions)))
    least = 1 if total - largest >= amount - 1 else 0
    holding, surplus = [largest] + [least] * (amount - 1), total - largest - least * (amount - 1)
    while surplus > 0:
        movable = [i for i in range(1, amount) if holding[i] < largest] or [i for i in range(1, amount) if holding[i] < reach]
        whole, budget = sum([portions[i] for i in movable]), surplus
        for i in movable:
            extra = min(reach - holding[i], max(1, budget * portions[i] // whole), surplus)
            holding[i] = holding[i] + extra
            surplus = surplus - extra
    return np.array(holding)


def noise(own_key, extent, deviation, limit, shards=(), kind=jnp.bfloat16):
    values = jax.random.normal(own_key, extent, jnp.float32) * deviation
    if len(shards) > 0:
        values = level_of(own_key, extent, shards, -0.22, 0.18) * values
    return jnp.clip(values, min=-limit, max=limit).astype(kind)


def setup_inputs(seed: int = 0) -> dict:
    streams_of = jax.random.split(jax.random.key(seed), 9)
    features = noise(streams_of[0], (H, NODES), 1.0, 6.0, ((0, 4), (1, 128)))
    near_tiles = draw_near_tiles(jax.random.fold_in(streams_of[8], 71), 0)
    far_tiles = draw_far_tiles(jax.random.fold_in(streams_of[8], 71), 0)
    far_source_keys = jax.random.split(jax.random.fold_in(streams_of[3], 1), FAR_ALL // FAR)
    far_source_turns = jax.random.permutation(jax.random.fold_in(streams_of[3], 3), FAR_ALL // FAR)
    far_source = jax.vmap(lambda own, number: assign_block(jax.random.fold_in(streams_of[3], 2), own, number, FAR, N_BLK, 1, MOST, 2))(far_source_keys, far_source_turns).reshape((FAR_ALL, 1))
    far_index = touch_ends(jax.random.randint(streams_of[4], (FAR_ALL, 2), 0, TPD), jax.random.fold_in(streams_of[4], 1), 0, TPD - 1).astype(jnp.int32)
    weight = noise(streams_of[5], (H, H), H ** -0.5, 0.375, ((1, 4),))
    bias = noise(streams_of[6], (H,), 0.5, 3.0, ((0, 4),), jnp.float32)
    grad_out = noise(streams_of[7], (H, NODES), 1.0, 6.0, ((0, 4), (1, 128)))
    return dict(features=features, near_tiles=near_tiles, far_tiles=far_tiles, far_source=far_source, far_index=far_index, weight=weight, bias=bias, grad_out=grad_out)


def reference(features, near_tiles, far_tiles, far_source, far_index, weight, bias, grad_out):
    offsets = jnp.arange(-3, 4, dtype=jnp.int32)
    feature_blocks = features.reshape(H, N_BLK, ROWS)
    feature_tiles = features.reshape(H, N_BLK * TPD, TILE)
    near_all = near_tiles.reshape(N_BLK, ROWS, 7, ROWS)
    far_all = far_tiles.reshape(N_BLK, FAR, TILE, TILE)
    sources = far_source.reshape(N_BLK, FAR).astype(jnp.int32)
    own_tiles = far_index[:, 0].reshape(N_BLK, FAR).astype(jnp.int32)
    src_tiles = far_index[:, 1].reshape(N_BLK, FAR).astype(jnp.int32)
    devices = jnp.arange(N_BLK, dtype=jnp.int32)

    def forward_block(inputs):
        device, near_block, far_block, source, own_tile, src_tile = inputs
        columns = (device + offsets) % N_BLK
        neighbours = jnp.take(feature_blocks, columns, axis=1).astype(jnp.float32)
        near_sum = jnp.einsum('hsb,asb->ha', neighbours, near_block.astype(jnp.float32))
        far_inputs = jnp.take(feature_tiles, source * TPD + src_tile, axis=1).astype(jnp.float32)
        partial_value = jnp.einsum('hkb,kab->kha', far_inputs, far_block.astype(jnp.float32))
        far_sum = jnp.zeros((TPD, H, TILE), jnp.float32).at[own_tile].add(partial_value)
        return near_sum + jnp.transpose(far_sum, (1, 0, 2)).reshape(H, ROWS)

    blocks_out = lax.map(forward_block, (devices, near_all, far_all, sources, own_tiles, src_tiles))
    aggregated = jnp.transpose(blocks_out, (1, 0, 2)).reshape(H, NODES).astype(jnp.bfloat16)
    pre_act = jnp.dot(weight.T, aggregated, preferred_element_type=jnp.float32) + bias[:, None]
    activated = jax.nn.silu(pre_act).astype(jnp.bfloat16)
    sigmoid_pre = jax.nn.sigmoid(pre_act)
    grad_pre = (grad_out.astype(jnp.float32) * sigmoid_pre * (1.0 + pre_act * (1.0 - sigmoid_pre))).astype(jnp.bfloat16)
    grad_weight = jnp.dot(aggregated, grad_pre.T, preferred_element_type=jnp.float32)
    grad_bias = jnp.sum(grad_pre.astype(jnp.float32), axis=1)
    grad_agg = jnp.dot(weight, grad_pre, preferred_element_type=jnp.float32).astype(jnp.bfloat16)
    grad_blocks = jnp.transpose(grad_agg.reshape(H, N_BLK, ROWS), (1, 0, 2))
    tile_range = jnp.arange(TPD, dtype=jnp.int32)

    def backward_block(accumulated, inputs):
        device, near_block, far_block, source, own_tile, src_tile, grad_block = inputs
        grad_float = grad_block.astype(jnp.float32)
        partial_value = jnp.einsum('ha,asb->shb', grad_float, near_block.astype(jnp.float32))
        partial_value = jnp.transpose(partial_value.reshape(7, H, TPD, TILE), (0, 2, 1, 3)).reshape(7 * TPD, H, TILE)
        targets = ((((device + offsets) % N_BLK) * TPD)[:, None] + tile_range[None, :]).reshape(-1)
        accumulated = accumulated.at[targets].add(partial_value)
        chosen = jnp.take(grad_float.reshape(H, TPD, TILE), own_tile, axis=1)
        far_partial = jnp.einsum('hka,kab->khb', chosen, far_block.astype(jnp.float32)).astype(jnp.bfloat16)
        accumulated = accumulated.at[source * TPD + src_tile].add(far_partial.astype(jnp.float32))
        return accumulated, None

    start_acc = jnp.zeros((N_BLK * TPD, H, TILE), jnp.float32)
    accumulated, unused = lax.scan(backward_block, start_acc, (devices, near_all, far_all, sources, own_tiles, src_tiles, grad_blocks))
    grad_feat = jnp.transpose(accumulated, (1, 0, 2)).reshape(H, NODES).astype(jnp.bfloat16)
    return activated, grad_feat, grad_weight, grad_bias
```

```python
import functools

import jax
import jax.numpy as jnp
from jax import lax
from jax.experimental import pallas as pl
from jax.experimental.pallas import tpu as pltpu
from jax.sharding import PartitionSpec as P

NX, NZ, NY, NC = 4, 8, 2, 2
NB = NX * NZ * NY * NC
HALF = NB // NC
GROUP = NX * NY
FAR = 96
BAND = 7
NF = 4
HD = 64
TILE = 128
ROWS = 256
F32 = jnp.float32
BF16 = jnp.bfloat16
NN = (((1,), (0,)), ((), ()))
NT = (((1,), (1,)), ((), ()))
TN = (((0,), (0,)), ((), ()))
STEPS = (4, 3, -3, 2, -2, 1, -1, 0)


def dot(a, b, dims):
    return lax.dot_general(a, b, dims, preferred_element_type=F32)


def send(src, dst, sent, got, **where):
    return pltpu.make_async_remote_copy(
        src_ref=src, dst_ref=dst, send_sem=sent, recv_sem=got,
        device_id=where, device_id_type=pl.DeviceIdType.MESH,
    )


def rem(a, n):
    return lax.rem(a, jnp.int32(n))


def gather_blocks(own, X, me, sy, ry, sR, rR, sL, rL, sX, rX, sP, rP):
    x, z, y, core, at = me
    X[core * HALF + z * GROUP + x * NY + y] = own

    right, left = at(x, rem(z + 1, NZ), y, core), at(x, rem(z + NZ - 1, NZ), y, core)
    partner = at(x, z, y, 1 - core)
    mine = X.at[core * HALF + z * GROUP + x * NY + y]
    other = X.at[core * HALF + z * GROUP + x * NY + 1 - y]
    swap = send(mine, mine, sy, ry, blk=at(x, z, 1 - y, core))
    swap.start()
    send(other, other, sy, ry, blk=at(x, z, 1 - y, core)).wait_recv()

    def piece(k, xx, zz):
        return X.at[pl.ds(k * HALF + zz * GROUP + xx * NY, NY)]

    def part(k, xx, zz, yy):
        return X.at[pl.ds(k * HALF + zz * GROUP + xx * NY + yy, 1)]

    def to_partner(ref):
        send(ref, ref, sP, rP, blk=partner).start()

    def ring_step(k, xx, i, s, start):
        zr, zl = rem(z + NZ - s, NZ), rem(z + s, NZ)
        for zz, sem_s, sem_r, to, yy in ((zr, sR, rR, right, 0), (zl, sL, rL, left, 1)):
            if s > 0:
                ref = piece(k, xx, zz) if s < 4 else part(k, xx, zz, yy)
                send(ref, ref, sem_s.at[i, s - 1], sem_r.at[i, s - 1], blk=to).wait_recv()
            if s < 4:
                ref = piece(k, xx, zz) if s < 3 else part(k, xx, zz, yy)
                send(ref, ref, sem_s.at[i, s], sem_r.at[i, s], blk=to).start()

    def ring_sent(k, xx, i):
        for s in range(4):
            zr, zl = rem(z + NZ - s, NZ), rem(z + s, NZ)
            for zz, sem_s, sem_r, to, yy in ((zr, sR, rR, right, 0), (zl, sL, rL, left, 1)):
                ref = piece(k, xx, zz) if s < 3 else part(k, xx, zz, yy)
                send(ref, ref, sem_s.at[i, s], sem_r.at[i, s], blk=to).wait_send()

    def x_peer(d):
        return at(rem(x + d, NX), z, y, core)

    @pl.when(core == 0)
    def _():
        def spread(zz, j):
            ref = piece(0, x, zz)
            for d in (1, 3, 2):
                send(ref, ref, sX.at[d - 1, j], rX.at[d - 1, j], blk=x_peer(d)).start()
            to_partner(ref)

        def collect(zz, j):
            for d in (1, 3, 2):
                ref = piece(0, rem(x + NX - d, NX), zz)
                send(ref, ref, sX.at[d - 1, j], rX.at[d - 1, j], blk=x_peer(d)).wait_recv()
                to_partner(ref)

        places = [z] + [rem(z + o, NZ) for s in (1, 2, 3) for o in (NZ - s, s)] + [rem(z + 4, NZ)]
        steps = [[0], [1, 2], [3, 4], [5, 6], [7]]
        for s in range(5):
            ring_step(0, x, 0, s, None)
            for j in steps[s]:
                spread(places[j], j)
            if s > 0:
                for j in steps[s - 1]:
                    collect(places[j], j)
        collect(places[7], 7)
        ring_sent(0, x, 0)
        for j in range(8):
            for d in (1, 3, 2):
                ref = piece(0, x, places[j])
                send(ref, ref, sX.at[d - 1, j], rX.at[d - 1, j], blk=x_peer(d)).wait_send()

    @pl.when(core == 1)
    def _():
        ref = piece(1, x, z)
        for d in (1, 3, 2):
            send(ref, ref, sX.at[d - 1, 0], rX.at[d - 1, 0], blk=x_peer(d)).start()
        ring_step(1, x, 0, 0, None)
        to_partner(ref)
        for d in (1, 3, 2):
            xx = rem(x + NX - d, NX)
            got = piece(1, xx, z)
            send(got, got, sX.at[d - 1, 0], rX.at[d - 1, 0], blk=x_peer(d)).wait_recv()
            ring_step(1, xx, d, 0, None)
            to_partner(got)
        for s in range(1, 5):
            zr, zl = rem(z + NZ - s, NZ), rem(z + s, NZ)
            for i in (0, 1, 3, 2):
                xx = rem(x + NX - i, NX)
                ring_step(1, xx, i, s, None)
                to_partner(piece(1, xx, zr))
                if s < 4:
                    to_partner(piece(1, xx, zl))
        for i in range(4):
            ring_sent(1, rem(x + NX - i, NX), i)
        for d in (1, 3, 2):
            send(ref, ref, sX.at[d - 1, 0], rX.at[d - 1, 0], blk=x_peer(d)).wait_send()

    whole, theirs = X.at[pl.ds(core * HALF, HALF)], X.at[pl.ds((1 - core) * HALF, HALF)]
    swap.wait_send()
    send(theirs, theirs, sP, rP, blk=partner).wait_recv()
    send(whole, whole, sP, rP, blk=partner).wait_send()


def to_feat(S, f, sent, got):
    copies = []
    for d in (1, 2, 3):
        copies.append(send(S.at[f], S.at[f], sent.at[d - 1], got.at[d - 1], feat=rem(f + d, NF)))
        copies[-1].start()
    return copies


def from_feat(S, f, sent, got):
    for d in (1, 2, 3):
        ref = S.at[rem(f + NF - d, NF)]
        send(ref, ref, sent.at[d - 1], got.at[d - 1], feat=rem(f + d, NF)).wait_recv()


def scatter_blocks(G, H, XR, RR, RL, Fs, Fr, out, me, hooks, sH, rH, sX, rX, sR, rR, sL, rL, sy, ry):
    x, z, y, core, at = me
    right, left = at(x, rem(z + 1, NZ), y, core), at(x, rem(z + NZ - 1, NZ), y, core)
    partner = at(x, z, y, 1 - core)
    zs = [rem(z + o + NZ, NZ) for o in STEPS]
    mine, theirs = core * HALF, (1 - core) * HALF

    def given(j):
        return send(
            G.at[pl.ds(theirs + zs[j] * GROUP, GROUP)], H.at[pl.ds(zs[j] * GROUP, GROUP)],
            sH.at[j], rH.at[j], blk=partner,
        )

    def taken(j):
        ref = H.at[pl.ds(zs[j] * GROUP, GROUP)]
        send(ref, ref, sH.at[j], rH.at[j], blk=partner).wait_recv()
        def body(n, _):
            g = zs[j] * GROUP + n
            G[mine + g] = (G[mine + g].astype(F32) + H[g].astype(F32)).astype(BF16)
            return 0
        lax.fori_loop(0, GROUP, body, 0)

    for j in range(8):
        given(j).start()

    def x_peer(d):
        return at(rem(x + d, NX), z, y, core)

    def ring_copy(xx, i, j, way):
        base = mine + zs[j] * GROUP + xx * NY
        R, to, ss, rr, yy = (RR, right, sR, rR, 0) if way == 0 else (RL, left, sL, rL, 1)
        step = (j + 1) // 2
        if j == 0:
            return send(G.at[pl.ds(base + yy, 1)], R.at[0, i, pl.ds(yy, 1)], ss.at[i, 0], rr.at[i, 0], blk=to)
        return send(G.at[pl.ds(base, NY)], R.at[step, i], ss.at[i, step], rr.at[i, step], blk=to)

    def ring_wait(i, step, way):
        R, to, ss, rr, yy = (RR, right, sR, rR, 0) if way == 0 else (RL, left, sL, rL, 1)
        ref = R.at[0, i, pl.ds(yy, 1)] if step == 0 else R.at[step, i]
        send(ref, ref, ss.at[i, step], rr.at[i, step], blk=to).wait_recv()

    def ring(xx, i, j):
        base = mine + zs[j] * GROUP + xx * NY
        if j == 0:
            ring_copy(xx, i, 0, 0).start()
            ring_copy(xx, i, 0, 1).start()
        elif j < 7:
            way, step = (0, (j - 1) // 2) if j % 2 else (1, (j - 2) // 2)
            R = RR if way == 0 else RL
            ring_wait(i, step, way)
            if step == 0:
                G[base + way] = (G[base + way].astype(F32) + R[0, i, way].astype(F32)).astype(BF16)
            else:
                for n in range(NY):
                    G[base + n] = (G[base + n].astype(F32) + R[step, i, n].astype(F32)).astype(BF16)
            ring_copy(xx, i, j, way).start()
        else:
            ring_wait(i, 3, 0)
            ring_wait(i, 3, 1)

    def ring_total(xx, i, n):
        base = mine + zs[7] * GROUP + xx * NY
        return G[base + n].astype(F32) + RR[3, i, n].astype(F32) + RL[3, i, n].astype(F32)

    def ring_sent(xx, i):
        ring_copy(xx, i, 0, 0).wait_send()
        ring_copy(xx, i, 0, 1).wait_send()
        for j in range(1, 7):
            ring_copy(xx, i, j, 0 if j % 2 else 1).wait_send()

    def x_copy(d, j):
        src = G.at[pl.ds(mine + zs[j] * GROUP + rem(x + d, NX) * NY, NY)]
        return send(src, XR.at[d - 1, j], sX.at[d - 1, j], rX.at[d - 1, j], blk=x_peer(d))

    def x_wait(j):
        for d in (1, 3, 2):
            ref = XR.at[d - 1, j]
            send(ref, ref, sX.at[d - 1, j], rX.at[d - 1, j], blk=x_peer(d)).wait_recv()

    def x_total(start, j, n):
        return start + XR[0, j, n].astype(F32) + XR[1, j, n].astype(F32) + XR[2, j, n].astype(F32)

    @pl.when(core == 0)
    def _():
        def along_z(j):
            x_wait(j)
            base = mine + zs[j] * GROUP + x * NY
            for n in range(NY):
                G[base + n] = x_total(G[base + n].astype(F32), j, n).astype(BF16)
            ring(x, 0, j)

        for j in range(8):
            taken(j)
            for d in (1, 3, 2):
                x_copy(d, j).start()
            if j >= 2:
                along_z(j - 2)
        along_z(6)
        along_z(7)
        for n in range(NY):
            Fs[n] = ring_total(x, 0, n).astype(BF16)
        ring_sent(x, 0)
        for j in range(8):
            for d in (1, 3, 2):
                x_copy(d, j).wait_send()

    @pl.when(core == 1)
    def _():
        for j in range(8):
            taken(j)
            for i in range(4):
                ring(rem(x + i, NX), i, j)
                if j == 7:
                    for n in range(NY):
                        base = mine + zs[7] * GROUP + rem(x + i, NX) * NY
                        G[base + n] = ring_total(rem(x + i, NX), i, n).astype(BF16)
                    if i > 0:
                        x_copy(i, 7).start()
        x_wait(7)
        base = mine + zs[7] * GROUP + x * NY
        for n in range(NY):
            Fs[n] = x_total(G[base + n].astype(F32), 7, n).astype(BF16)
        for i in range(4):
            ring_sent(rem(x + i, NX), i)
        for d in (1, 3, 2):
            x_copy(d, 7).wait_send()

    last = send(Fs.at[1 - y], Fr, sy, ry, blk=at(x, z, 1 - y, core))
    last.start()
    last.wait()
    total = Fs[y].astype(F32) + Fr[...].astype(F32)
    out[:, 0:TILE] = total[0].astype(BF16)
    out[:, TILE:] = total[1].astype(BF16)
    for j in range(8):
        given(j).wait_send()


def kernel(
    feat_ref, near_hbm, far_hbm, place_ref, own_ref, table_ref, weight_ref, bias_ref, gout_ref,
    act_ref, gfeat_ref, gw_ref, gb_ref,
    near, far, X, G, H, XR, RR, RL, Fs, Fr, A, GP, WR, ga, parts, band,
    W0, W1, W2, W3, W5, W7, W8,
    local, sy, ry, sR, rR, sL, rL, sX, rX, sP, rP,
    sf, rf, sH, rH, tX, uX, tR, uR, tL, uL, sw, rw, sz, rz, sq, rq, sz2, rz2,
):
    b, f = lax.axis_index("blk"), lax.axis_index("feat")
    core, y, z, x = b % 2, (b // 2) % 2, (b // 4) % 8, b // 32

    def at(xx, zz, yy, cc):
        return ((xx * NZ + zz) * NY + yy) * NC + cc

    me = (x, z, y, core, at)
    partner = at(x, z, y, 1 - core)

    def slab(e):
        return rem(x + e // 2, NX), (y + e % 2) % 2

    load_far = pltpu.make_async_copy(far_hbm, far, local.at[0])
    load_near = pltpu.make_async_copy(near_hbm, near, local.at[1])
    load_far.start()
    load_near.start()

    barrier = pltpu.get_barrier_semaphore()
    for d in range(1, NZ):
        pl.semaphore_signal(barrier, 1, device_id={"blk": at(x, rem(z + d, NZ), y, core)}, device_id_type=pl.DeviceIdType.MESH)
    for e in range(1, 8):
        xx, yy = slab(e)
        pl.semaphore_signal(barrier, 1, device_id={"blk": at(xx, z, yy, core)}, device_id_type=pl.DeviceIdType.MESH)
    pl.semaphore_signal(barrier, 1, device_id={"blk": partner}, device_id_type=pl.DeviceIdType.MESH)
    for d in (1, 2, 3):
        pl.semaphore_signal(barrier, 1, device_id={"feat": rem(f + d, NF)}, device_id_type=pl.DeviceIdType.MESH)
    pl.semaphore_wait(barrier, 18)

    rows = []
    for d in (1, 2, 3):
        to = rem(f + d, NF)
        rows.append(send(weight_ref.at[pl.ds(pl.multiple_of(to * HD, HD), HD)], WR.at[f], sf.at[0, d - 1], rf.at[0, d - 1], feat=to))
        rows[-1].start()
    WR[f] = weight_ref[pl.ds(pl.multiple_of(f * HD, HD), HD), :]

    own = jnp.stack([feat_ref[:, 0:TILE], feat_ref[:, TILE:]])
    gather_blocks(own, X, me, sy.at[0], ry.at[0], sR, rR, sL, rL, sX, rX, sP, rP)

    load_near.wait()
    load_far.wait()
    total = jnp.zeros((HD, ROWS), F32)
    for s in range(BAND):
        c = rem(b + NB + s - 3, NB)
        spot = (c % 2) * HALF + ((c // 4) % 8) * GROUP + (c // 32) * NY + (c // 2) % 2
        total += dot(jnp.concatenate([X[spot, 0], X[spot, 1]], axis=1), near[s], NT)

    def far_forward(n, sums):
        low, high = sums
        for r in range(8):
            q = n * 8 + r
            p = place_ref[q]
            value = dot(X[p // 2, p % 2], far[q], NT)
            first = own_ref[q] == 0
            low += jnp.where(first, value, 0.0)
            high += jnp.where(first, 0.0, value)
        return low, high

    zero = jnp.zeros((HD, TILE), F32)
    low, high = lax.fori_loop(0, FAR // 8, far_forward, (zero, zero))
    A[f] = (total + jnp.concatenate([low, high], axis=1)).astype(BF16)
    first = to_feat(A, f, sf.at[1], rf.at[1])
    from_feat(A, f, sf.at[1], rf.at[1])

    gathered = A[...].reshape(NF * HD, ROWS)
    pre = dot(weight_ref[...], gathered, TN) + bias_ref[...]
    sig = jax.nn.sigmoid(pre)
    grad_pre = (gout_ref[...].astype(F32) * sig * (1.0 + pre * (1.0 - sig))).astype(BF16)
    GP[f] = grad_pre
    second = to_feat(GP, f, sf.at[2], rf.at[2])
    act_ref[...] = (pre * sig).astype(BF16)
    part = dot(gathered, grad_pre, NT)
    ones = dot(jnp.ones((8, ROWS), BF16), grad_pre, NT)
    W0[:, :, 0:8, 0:HD] = part[0:128].reshape(2, 8, 8, HD)
    W0[:, :, 0:8, HD:] = part[128:256].reshape(2, 8, 8, HD)
    side = jnp.concatenate([ones, ones], axis=1)
    for k in range(2):
        for n in range(8):
            W0[k, n, 8:16, :] = side
    halves = send(W0.at[1 - core], W1, sw.at[0], rw.at[0], blk=partner)
    halves.start()
    for d in (1, 2, 3):
        ref = WR.at[rem(f + NF - d, NF)]
        send(ref, ref, sf.at[0, d - 1], rf.at[0, d - 1], feat=rem(f + d, NF)).wait_recv()
    from_feat(GP, f, sf.at[2], rf.at[2])
    grad = jnp.zeros((HD, ROWS), F32)
    for n in range(NF):
        grad += dot(WR[n], GP[n], NN)
    grad = grad.astype(BF16)
    ga[0] = grad[:, 0:TILE]
    ga[1] = grad[:, TILE:]

    def far_backward(n, _):
        for r in range(8):
            q = n * 8 + r
            parts[q] = dot(ga[own_ref[q]], far[q], NN).astype(BF16)
        return 0

    lax.fori_loop(0, FAR // 8, far_backward, 0)
    parts[FAR] = jnp.zeros((HD, TILE), BF16)
    for s in range(BAND):
        value = dot(grad, near[s], NN)
        band[s, 0] = value[:, 0:TILE]
        band[s, 1] = value[:, TILE:]

    halves.wait()
    W2[...] = W0[core] + W1[...]
    to_z = []
    for d in range(1, NZ):
        zz = rem(z + d, NZ)
        to_z.append(send(W2.at[zz], W3.at[d - 1], sz.at[d - 1], rz.at[d - 1], blk=at(x, zz, y, core)))
        to_z[-1].start()

    def place(n, _):
        for r in range(4):
            c = n * 4 + r
            one, two = table_ref[0, c], table_ref[1, c]
            va, vb = parts[one // 2].astype(F32), parts[two // 2].astype(F32)
            ua, ub = one % 2 == 0, two % 2 == 0
            G[c, 0] = (jnp.where(ua, va, 0.0) + jnp.where(ub, vb, 0.0)).astype(BF16)
            G[c, 1] = (jnp.where(ua, 0.0, va) + jnp.where(ub, 0.0, vb)).astype(BF16)
        return 0

    lax.fori_loop(0, NB // 4, place, 0)
    for s in range(BAND):
        c = rem(b + NB + s - 3, NB)
        spot = (c % 2) * HALF + ((c // 4) % 8) * GROUP + (c // 32) * NY + (c // 2) % 2
        G[spot] = (G[spot].astype(F32) + band[s]).astype(BF16)

    for copy in to_z:
        copy.wait()
    mine = W2[z]
    for d in range(NZ - 1):
        mine += W3[d]
    W5[x * NY + y] = mine
    to_slab = []
    for e in range(1, 8):
        xx, yy = slab(e)
        to_slab.append(send(W5.at[x * NY + y], W5.at[x * NY + y], sq.at[e - 1], rq.at[e - 1], blk=at(xx, z, yy, core)))
        to_slab[-1].start()

    scatter_blocks(G, H, XR, RR, RL, Fs, Fr, gfeat_ref, me, None, sH, rH, tX, uX, tR, uR, tL, uL, sy.at[1], ry.at[1])

    for e in range(1, 8):
        xx, yy = rem(x + NX - e // 2, NX), (y + e % 2) % 2
        ref = W5.at[xx * NY + yy]
        send(ref, ref, sq.at[e - 1], rq.at[e - 1], blk=partner).wait_recv()
    total = W5[0]
    for n in range(1, 8):
        total += W5[n]
    W7[z] = total
    again = []
    for d in range(1, NZ):
        again.append(send(W7.at[z], W7.at[z], sz2.at[d - 1], rz2.at[d - 1], blk=at(x, rem(z + d, NZ), y, core)))
        again[-1].start()
    for d in range(1, NZ):
        ref = W7.at[rem(z + NZ - d, NZ)]
        send(ref, ref, sz2.at[d - 1], rz2.at[d - 1], blk=partner).wait_recv()
    final = send(W7, W8, sw.at[1], rw.at[1], blk=partner)
    final.start()
    final.wait_recv()
    for k in range(2):
        here = (k == core)
        value = jnp.where(here, W7[...], W8[...])
        rows_of = value[:, 0:8, :].reshape(64, 2 * HD)
        gw_ref[k * 64:k * 64 + 64, :] = rows_of[:, 0:HD]
        gw_ref[128 + k * 64:128 + k * 64 + 64, :] = rows_of[:, HD:]
    both = jnp.where(core == 0, W7[0, 8:16, :], W8[0, 8:16, :])
    gb_ref[...] = both[:, 0:HD]

    for copy in rows + first + second + to_slab + again:
        copy.wait_send()
    final.wait_send()


def on_device(features, near_tiles, far_tiles, far_source, far_index, weight, bias, grad_out):
    near = jnp.transpose(near_tiles, (1, 0, 2))
    c = far_source[:, 0]
    spot = (c % 2) * HALF + ((c // 4) % 8) * GROUP + (c // 32) * NY + (c // 2) % 2
    place = spot * 2 + far_index[:, 1]
    key = jnp.arange(FAR, dtype=jnp.int32) * 2 + far_index[:, 1]
    match = spot[None, :] == jnp.arange(NB, dtype=jnp.int32)[:, None]
    one = jnp.min(jnp.where(match, key[None, :], 2 * FAR), axis=1)
    two = jnp.max(jnp.where(match, key[None, :], -1), axis=1)
    two = jnp.where((two == one) | (two < 0), 2 * FAR, two)
    table = jnp.stack([one, two])
    vmem, smem, any_ = (pl.BlockSpec(memory_space=s) for s in (pltpu.VMEM, pltpu.SMEM, pl.ANY))
    dma = lambda *shape: pltpu.SemaphoreType.DMA(shape)
    block = (2, HD, TILE)
    act, gfeat, gw, gb = pl.pallas_call(
        kernel,
        out_shape=(
            jax.ShapeDtypeStruct((HD, ROWS), BF16),
            jax.ShapeDtypeStruct((HD, ROWS), BF16),
            jax.ShapeDtypeStruct((NF * HD, HD), F32),
            jax.ShapeDtypeStruct((8, HD), F32),
        ),
        in_specs=[vmem, any_, any_, smem, smem, smem, vmem, vmem, vmem],
        out_specs=(vmem,) * 4,
        scratch_shapes=[
            pltpu.VMEM((BAND, ROWS, ROWS), BF16),
            pltpu.VMEM((FAR, TILE, TILE), BF16),
            pltpu.VMEM((NB,) + block, BF16),
            pltpu.VMEM((NB,) + block, BF16),
            pltpu.VMEM((HALF,) + block, BF16),
            pltpu.VMEM((3, 8, NY) + block, BF16),
            pltpu.VMEM((4, NX, NY) + block, BF16),
            pltpu.VMEM((4, NX, NY) + block, BF16),
            pltpu.VMEM((NY,) + block, BF16),
            pltpu.VMEM(block, BF16),
            pltpu.VMEM((NF, HD, ROWS), BF16),
            pltpu.VMEM((NF, HD, ROWS), BF16),
            pltpu.VMEM((NF, HD, HD), BF16),
            pltpu.VMEM(block, BF16),
            pltpu.VMEM((FAR + 1, HD, TILE), BF16),
            pltpu.VMEM((BAND,) + block, F32),
            pltpu.VMEM((2, 8, 16, 128), F32),
            pltpu.VMEM((8, 16, 128), F32),
            pltpu.VMEM((8, 16, 128), F32),
            pltpu.VMEM((7, 16, 128), F32),
            pltpu.VMEM((8, 16, 128), F32),
            pltpu.VMEM((8, 16, 128), F32),
            pltpu.VMEM((8, 16, 128), F32),
            dma(2), dma(2), dma(2),
            dma(4, 4), dma(4, 4), dma(4, 4), dma(4, 4), dma(3, 8), dma(3, 8), pltpu.SemaphoreType.DMA, pltpu.SemaphoreType.DMA,
            dma(3, 3), dma(3, 3), dma(8), dma(8), dma(3, 8), dma(3, 8),
            dma(4, 4), dma(4, 4), dma(4, 4), dma(4, 4), dma(2), dma(2), dma(7), dma(7), dma(7), dma(7), dma(7), dma(7),
        ],
        compiler_params=pltpu.CompilerParams(
            collective_id=0, has_side_effects=True, vmem_limit_bytes=40 * 2**20
        ),
    )(features, near, far_tiles, place, far_index[:, 0], table, weight, bias[:, None], grad_out)
    return act, gfeat, gw, gb[0]


def solution(mesh):
    return jax.shard_map(
        on_device,
        mesh=mesh,
        in_specs=(
            P("feat", "blk"),
            P("blk", None, None),
            P("blk", None, None),
            P("blk", None),
            P("blk", None),
            P(None, "feat"),
            P("feat"),
            P("feat", "blk"),
        ),
        out_specs=(P("feat", "blk"), P("feat", "blk"), P(None, "feat"), P("feat")),
        check_vma=False,
    )
```

```python
import functools

import jax
import jax.numpy as jnp
from jax import lax
from jax.experimental import pallas as pl
from jax.experimental.pallas import tpu as pltpu
from jax.sharding import PartitionSpec as P

NX, NZ, NY, NC = 4, 8, 2, 2
NB = NX * NZ * NY * NC
HALF = NB // NC
GROUP = NX * NY
FAR = 96
BAND = 7
NF = 4
HD = 64
TILE = 128
ROWS = 256
F32 = jnp.float32
BF16 = jnp.bfloat16
NN = (((1,), (0,)), ((), ()))
NT = (((1,), (1,)), ((), ()))
TN = (((0,), (0,)), ((), ()))
STEPS = (4, 3, -3, 2, -2, 1, -1, 0)


def dot(a, b, dims):
    return lax.dot_general(a, b, dims, preferred_element_type=F32)


def send(src, dst, sent, got, **where):
    return pltpu.make_async_remote_copy(
        src_ref=src, dst_ref=dst, send_sem=sent, recv_sem=got,
        device_id=where, device_id_type=pl.DeviceIdType.MESH,
    )


def rem(a, n):
    return lax.rem(a, jnp.int32(n))


def within(n, most):
    return jnp.minimum(jnp.maximum(n, 0), most)


def spot_of(c):
    return (c % 2) * HALF + ((c // 4) % 8) * GROUP + ((c // 2) % 2) * NX + c // 32


def gather_blocks(X, me, sy, ry, sR, rR, sL, rL, sXR, rXR, sXL, rXL, sP, rP):
    x, z, y, core, at = me
    east, west = at(rem(x + 1, NX), z, y, core), at(rem(x + NX - 1, NX), z, y, core)
    partner, across = at(x, z, y, 1 - core), at(x, z, 1 - y, core)
    ys = (y, 1 - y)

    def block(k, xx, zz, w):
        return k * HALF + zz * GROUP + ys[w] * NX + xx

    def whole(k, xx, zz, w):
        return X.at[block(k, xx, zz, w)]

    swap = send(whole(core, x, z, 0), whole(core, x, z, 0), sy, ry, blk=across)
    swap.start()

    def swapped():
        send(whole(core, x, z, 1), whole(core, x, z, 1), sy, ry, blk=across).wait_recv()

    def hand(k, zz, w, wait=False):
        ref = X.at[pl.ds(k * HALF + zz * GROUP + ys[w] * NX, NX)]
        copy = send(ref, ref, sP, rP, blk=partner)
        copy.start()

    def ring_parts(k, xx, i, w, wide):
        out = []
        for sign, ss, rr in ((1, sR, rR), (-1, sL, rL)):
            def step(n, zd, hops, half, ss=ss, rr=rr, sign=sign):
                src = whole(k, xx, rem(z + NZ - sign * zd, NZ), w)
                src = src if half is None else src.at[half]
                return send(src, src, ss.at[w, i, n], rr.at[w, i, n], blk=at(x, rem(z + NZ + sign * hops, NZ), y, core))

            half = 0 if sign == 1 else 1
            out.append((
                functools.partial(step, 0, 0, 1, None),
                functools.partial(step, 1, 0, 2, None) if wide else functools.partial(step, 1, 1, 1, None),
                functools.partial(step, 2, 2, 1, None),
                functools.partial(step, 3, 2, 2, half),
            ))
        return out

    def ring_got(k, xx, i, w, n):
        for sign, ss, rr, u in ((1, sR, rR, 0), (-1, sL, rL, 1)):
            ref = whole(k, xx, rem(z + NZ - sign * (n + 1), NZ), w)
            ref = ref if n < 3 else ref.at[u]
            send(ref, ref, ss.at[w, i, n], rr.at[w, i, n], blk=partner).wait_recv()

    def ring_start(k, xx, i, w, wide):
        parts = ring_parts(k, xx, i, w, wide)
        if wide:
            parts[0][1]().start()
            parts[1][1]().start()
        parts[0][0]().start()
        parts[1][0]().start()

    def ring_second(k, xx, i, w):
        ring_got(k, xx, i, w, 0)
        for part in ring_parts(k, xx, i, w, False):
            part[1]().start()

    def ring_third(k, xx, i, w):
        ring_got(k, xx, i, w, 1)
        for part in ring_parts(k, xx, i, w, True):
            part[3]().start()
            part[2]().start()

    def ring_sent(k, xx, i, w, wide):
        for part in ring_parts(k, xx, i, w, wide):
            for copy in part:
                copy().wait_send()

    def x_step(k, zz, j, w, s, what):
        for xx, ss, rr, to, u in ((rem(x + NX - s, NX), sXR, rXR, east, 0), (rem(x + s, NX), sXL, rXL, west, 1)):
            ref = whole(k, xx, zz, w)
            if what == "go" and s > 0:
                got = ref if s < 2 else ref.at[u]
                send(got, got, ss.at[w, j, s - 1], rr.at[w, j, s - 1], blk=to).wait_recv()
            if s < 2:
                out = ref if s < 1 else ref.at[u]
                copy = send(out, out, ss.at[w, j, s], rr.at[w, j, s], blk=to)
                copy.start() if what == "go" else copy.wait_send()

    def places(s):
        if s == 0:
            return [(z, 0)]
        if s == 4:
            return [(rem(z + 4, NZ), 7)]
        return [(rem(z + NZ - s, NZ), 2 * s - 1), (rem(z + s, NZ), 2 * s)]

    def across_x(w):
        ref = whole(1, x, z, w)
        return (
            send(ref, ref, sXR.at[w, 0, 0], rXR.at[w, 0, 0], blk=east),
            send(ref, ref, sXL.at[w, 0, 0], rXL.at[w, 0, 0], blk=west),
            send(ref, ref, sXR.at[w, 0, 1], rXR.at[w, 0, 1], blk=at(rem(x + 2, NX), z, y, core)),
        )

    def from_x(w, i):
        ref = whole(1, rem(x + NX - i, NX), z, w)
        ss, rr, n = ((sXR, rXR, 0), (sXR, rXR, 1), (sXL, rXL, 0))[i - 1]
        send(ref, ref, ss.at[w, 0, n], rr.at[w, 0, n], blk=partner).wait_recv()

    def hop(s, w, n):
        for zz, j in places(s):
            x_step(0, zz, j, w, n, "go")
            if n == 2:
                hand(0, zz, w)

    @pl.when(core == 0)
    def _():
        def got(n, w):
            ring_got(0, x, 0, w, n)
            hop(n + 1, w, 0)

        def third(w):
            ring_third(0, x, 0, w)
            hop(2, w, 0)

        ring_start(0, x, 0, 0, True)
        hop(0, 0, 0)
        third(0)
        got(0, 0)
        swapped()
        ring_start(0, x, 0, 1, True)
        hop(0, 1, 0)
        hop(0, 0, 1)
        got(2, 0)
        got(3, 0)
        hop(2, 0, 1)
        hop(1, 0, 1)
        hop(0, 0, 2)
        third(1)
        got(0, 1)
        for s, w, n in ((0, 1, 1), (3, 0, 1), (4, 0, 1), (2, 0, 2), (1, 0, 2)):
            hop(s, w, n)
        got(2, 1)
        got(3, 1)
        for s, w, n in (
            (2, 1, 1), (1, 1, 1), (3, 0, 2), (4, 0, 2), (0, 1, 2), (3, 1, 1), (4, 1, 1),
            (2, 1, 2), (1, 1, 2), (3, 1, 2), (4, 1, 2),
        ):
            hop(s, w, n)

    @pl.when(core == 1)
    def _():
        every = (0, 1, 3, 2)

        def xs(i):
            return rem(x + NX - i, NX)

        def spread(w):
            for i in (1, 3, 2):
                from_x(w, i)
                ring_start(1, xs(i), i, w, False)
            hand(1, z, w)

        def second(w, which):
            for i in which:
                ring_second(1, xs(i), i, w)

        def third(w, which):
            for i in which:
                ring_third(1, xs(i), i, w)

        def done(w, n):
            for i in every:
                ring_got(1, xs(i), i, w, n)
            for zz, j in places(n + 1):
                hand(1, zz, w)

        def along(w, n):
            for zz, j in places(n + 1):
                hand(1, zz, w)

        for copy in across_x(0):
            copy.start()
        ring_start(1, x, 0, 0, False)
        spread(0)
        second(0, (0,))
        swapped()
        for copy in across_x(1):
            copy.start()
        ring_start(1, x, 0, 1, False)
        second(0, (1, 3, 2))
        along(0, 0)
        third(0, (0,))
        spread(1)
        second(1, (0,))
        third(0, (1, 3, 2))
        along(0, 1)
        second(1, (1, 3, 2))
        along(1, 0)
        third(1, (0,))
        done(0, 2)
        done(0, 3)
        third(1, (1, 3, 2))
        along(1, 1)
        done(1, 2)
        done(1, 3)

    theirs = X.at[pl.ds((1 - core) * HALF, HALF)]
    send(theirs, theirs, sP, rP, blk=partner).wait_recv()

    def finish():
        swap.wait_send()
        ours = X.at[pl.ds(core * HALF, HALF)]
        send(ours, ours, sP, rP, blk=partner).wait_send()

        @pl.when(core == 0)
        def _():
            for w in (0, 1):
                ring_sent(0, x, 0, w, True)
                for s in range(5):
                    for zz, j in places(s):
                        x_step(0, zz, j, w, 0, "end")
                        x_step(0, zz, j, w, 1, "end")

        @pl.when(core == 1)
        def _():
            for w in (0, 1):
                for copy in across_x(w):
                    copy.wait_send()
                for i in range(4):
                    ring_sent(1, rem(x + NX - i, NX), i, w, False)

    return finish


def to_feat(S, f, sent, got):
    copies = []
    for d in (1, 2, 3):
        copies.append(send(S.at[f], S.at[f], sent.at[d - 1], got.at[d - 1], feat=rem(f + d, NF)))
        copies[-1].start()
    return copies


def from_feat(S, f, sent, got):
    for d in (1, 2, 3):
        ref = S.at[rem(f + NF - d, NF)]
        send(ref, ref, sent.at[d - 1], got.at[d - 1], feat=rem(f + d, NF)).wait_recv()


def add_to(G, at, u, *more):
    if u is None:
        total = G[at].astype(F32)
        for m in more:
            total += m.astype(F32)
        G[at] = total.astype(BF16)
    else:
        total = G[at, u].astype(F32)
        for m in more:
            total += m.astype(F32)
        G[at, u] = total.astype(BF16)


def scatter_blocks(G, H, XE, XW, RR, RL, Fs, Fr, out, me, hooks, sH, rH, sXR, rXR, sXL, rXL, sR, rR, sL, rL, sy, ry):
    x, z, y, core, at = me
    east, west = at(rem(x + 1, NX), z, y, core), at(rem(x + NX - 1, NX), z, y, core)
    partner, across = at(x, z, y, 1 - core), at(x, z, 1 - y, core)
    zs = [rem(z + o + NZ, NZ) for o in STEPS]
    ys = (1 - y, y)
    mine, theirs = core * HALF, (1 - core) * HALF

    def block(xx, j, w):
        return mine + zs[j] * GROUP + ys[w] * NX + xx

    def given(zz, yy, n):
        ref = G.at[pl.ds(theirs + zz * GROUP + yy * NX, NX)]
        return send(ref, H.at[pl.ds(zz * GROUP + yy * NX, NX)], sH.at[n], rH.at[n], blk=partner)

    def taken(j, w):
        base = zs[j] * GROUP + ys[w] * NX
        ref = H.at[pl.ds(base, NX)]
        send(ref, ref, sH.at[j * 2 + w], rH.at[j * 2 + w], blk=partner).wait_recv()
        for n in range(NX):
            add_to(G, mine + base + n, None, H[base + n])

    def ring_copy(xx, i, w, n, way, wide):
        R, ss, rr, sign = (RR, sR, rR, 1) if way == 0 else (RL, sL, rL, -1)
        src = G.at[mine + rem(z + NZ + sign * (n + 1), NZ) * GROUP + ys[w] * NX + xx]
        dst = R.at[w, n, i]
        if n == 3:
            src, dst = src.at[way], dst.at[way]
        hops = 2 if n == 3 or (n == 1 and wide) else 1
        return send(src, dst, ss.at[w, i, n], rr.at[w, i, n], blk=at(x, rem(z + NZ + sign * hops, NZ), y, core))

    def ring_wait(i, w, n, way):
        R, ss, rr = (RR, sR, rR) if way == 0 else (RL, sL, rL)
        ref = R.at[w, n, i, way] if n == 3 else R.at[w, n, i]
        send(ref, ref, ss.at[w, i, n], rr.at[w, i, n], blk=partner).wait_recv()

    def ring(xx, i, j, w, wide):
        if j == 0:
            for way in (0, 1):
                ring_copy(xx, i, w, 3, way, wide).start()
            return
        if j == 7:
            total = G[block(xx, 7, w)].astype(F32)
            for way, R in ((0, RR), (1, RL)):
                for n in (0, 1) if wide else (0,):
                    ring_wait(i, w, n, way)
                    total += R[w, n, i].astype(F32)
            return total
        way, n = (j + 1) % 2, 2 - (j - 1) // 2
        R, base = (RR, RL)[way], block(xx, j, w)
        if n == 1:
            ring_wait(i, w, 3, way)
            ring_wait(i, w, 2, way)
            add_to(G, base, way, R[w, 3, i, way])
            add_to(G, base, None, R[w, 2, i])
        if n == 0 and not wide:
            ring_wait(i, w, 1, way)
            add_to(G, base, None, R[w, 1, i])
        ring_copy(xx, i, w, n, way, wide).start()

    def ring_sent(xx, i, w, wide):
        for n in range(4):
            for way in (0, 1):
                ring_copy(xx, i, w, n, way, wide).wait_send()

    def x_copies(j, w, s):
        far, near_e, near_w = block(rem(x + 2, NX), j, w), block(rem(x + 1, NX), j, w), block(rem(x + NX - 1, NX), j, w)
        n = j * 2 + w
        if s == 0:
            return (send(G.at[far, 0], XE.at[n, 0, 0], sXR.at[n, 0], rXR.at[n, 0], blk=east),
                    send(G.at[far, 1], XW.at[n, 0, 1], sXL.at[n, 0], rXL.at[n, 0], blk=west))
        return (send(G.at[near_e], XE.at[n, 1], sXR.at[n, 1], rXR.at[n, 1], blk=east),
                send(G.at[near_w], XW.at[n, 1], sXL.at[n, 1], rXL.at[n, 1], blk=west))

    def x_step(j, w, s):
        n = j * 2 + w
        if s > 0:
            for copy in x_copies(j, w, s - 1):
                copy.wait_recv()
        if s == 1:
            add_to(G, block(rem(x + 1, NX), j, w), 0, XE[n, 0, 0])
            add_to(G, block(rem(x + NX - 1, NX), j, w), 1, XW[n, 0, 1])
        if s < 2:
            for copy in x_copies(j, w, s):
                copy.start()

    def x_total(j, w):
        n = j * 2 + w
        return G[block(x, j, w)].astype(F32) + XE[n, 1].astype(F32) + XW[n, 1].astype(F32)

    def across_x(w):
        n = 14 + w
        return (
            send(G.at[block(rem(x + 1, NX), 7, w)], XE.at[n, 1], sXR.at[n, 1], rXR.at[n, 1], blk=east),
            send(G.at[block(rem(x + NX - 1, NX), 7, w)], XW.at[n, 1], sXL.at[n, 1], rXL.at[n, 1], blk=west),
            send(G.at[block(rem(x + 2, NX), 7, w)], XE.at[n, 0], sXR.at[n, 0], rXR.at[n, 0], blk=at(rem(x + 2, NX), z, y, core)),
        )

    def from_x(w):
        for copy in across_x(w):
            copy.wait_recv()
        return x_total(7, w) + XE[14 + w, 0].astype(F32)

    order = tuple((j, w) for w in range(2) for j in range(8))
    last = send(Fs.at[0], Fr, sy, ry, blk=across)

    def deliver(w, total):
        Fs[w] = total.astype(BF16)
        if w == 0:
            last.start()

    def run():
        @pl.when(core == 0)
        def _():
            for n in range(len(order) + 8):
                if n < len(order):
                    taken(*order[n])
                    x_step(*order[n], 0)
                if 0 <= n - 4 < len(order):
                    x_step(*order[n - 4], 1)
                if 0 <= n - 8:
                    j, w = order[n - 8]
                    x_step(j, w, 2)
                    G[block(x, j, w)] = x_total(j, w).astype(BF16)
                    total = ring(x, 0, j, w, True)
                    if j == 7:
                        deliver(w, total)
                if n in hooks:
                    hooks[n]()

        @pl.when(core == 1)
        def _():
            for n, (j, w) in enumerate(order):
                taken(j, w)
                for i in (2, 1, 3, 0):
                    xx = rem(x + i, NX)
                    total = ring(xx, i, j, w, False)
                    if j == 7:
                        G[block(xx, 7, w)] = total.astype(BF16)
                if j == 7:
                    for copy in across_x(w):
                        copy.start()
                if (j, w) == (4, 1):
                    deliver(0, from_x(0))
                if (j, w) == (7, 1):
                    deliver(1, from_x(1))
                if n in hooks:
                    hooks[n]()

        last.wait_recv()
        total = Fs[1].astype(F32) + Fr[...].astype(F32)
        out[:, 0:TILE] = total[0].astype(BF16)
        out[:, TILE:] = total[1].astype(BF16)

    def finish():
        last.wait_send()
        for j in range(8):
            for w in range(2):
                given(zs[j], ys[w], j * 2 + w).wait_send()

        @pl.when(core == 0)
        def _():
            for w in range(2):
                ring_sent(x, 0, w, True)
                for j in range(8):
                    for s in range(2):
                        for copy in x_copies(j, w, s):
                            copy.wait_send()

        @pl.when(core == 1)
        def _():
            for w in range(2):
                for i in range(4):
                    ring_sent(rem(x + i, NX), i, w, False)
                for copy in across_x(w):
                    copy.wait_send()

    return given, run, finish


def kernel(
    feat_hbm, near_hbm, far_hbm, source_ref, index_ref, source_row, index_row, weight_hbm, bias_ref, gout_hbm,
    act_ref, gfeat_ref, gw_ref, gb_ref,
    near, far, feat_in, gout_in, X, G, H, XE, XW, RR, RL, Fs, Fr, A, GP, WR, WT, ga, parts, band, rows_v, table,
    W0, W1, W2, W3, W5, W7, W8,
    local, sy, ry, sR, rR, sL, rL, sXR, rXR, sXL, rXL, sP, rP,
    sf, rf, sH, rH, tXR, uXR, tXL, uXL, tR, uR, tL, uL, sw, rw, sz, rz, sq, rq, sz2, rz2,
):
    b, f = lax.axis_index("blk"), lax.axis_index("feat")
    core, y, z, x = b % 2, (b // 2) % 2, (b // 4) % 8, b // 32

    def at(xx, zz, yy, cc):
        return ((xx * NZ + zz) * NY + yy) * NC + cc

    me = (x, z, y, core, at)
    partner = at(x, z, y, 1 - core)

    def slab(e):
        return rem(x + e // 2, NX), (y + e % 2) % 2

    def signal(**where):
        pl.semaphore_signal(barrier, 1, device_id=where, device_id_type=pl.DeviceIdType.MESH)

    barrier = pltpu.get_barrier_semaphore()
    signal(blk=partner)
    for e in range(1, 8):
        xx, yy = slab(e)
        signal(blk=at(xx, z, yy, core))
    for d in range(1, NZ):
        signal(blk=at(x, rem(z + d, NZ), y, core))
    for d in (1, 2, 3):
        signal(feat=rem(f + d, NF))

    load_feat = pltpu.make_async_copy(feat_hbm, feat_in, local.at[0])
    load_weight = pltpu.make_async_copy(weight_hbm, WR.at[f], local.at[1])
    load_gout = pltpu.make_async_copy(gout_hbm, gout_in, local.at[2])
    load_near = pltpu.make_async_copy(near_hbm, near, local.at[3])
    load_far = pltpu.make_async_copy(far_hbm, far, local.at[4])
    for load in (load_feat, load_weight, load_gout, load_near, load_far):
        load.start()

    places = jnp.broadcast_to(spot_of(source_row[...]), (NB, FAR))
    keys = jnp.broadcast_to((lax.broadcasted_iota(jnp.int32, (1, FAR), 1) * 2 + index_row[1:2, :]).astype(F32), (NB, FAR))
    match = places == lax.broadcasted_iota(jnp.int32, (NB, FAR), 0)
    one = jnp.min(jnp.where(match, keys, 2.0 * FAR), axis=1, keepdims=True)
    two = jnp.max(jnp.where(match, keys, -1.0), axis=1, keepdims=True)
    two = jnp.where((two == one) | (two < 0.0), 2.0 * FAR, two)
    rows_v[0:8] = jnp.transpose(jnp.broadcast_to(one, (NB, NB)))[0:8].astype(jnp.int32)
    rows_v[8:16] = jnp.transpose(jnp.broadcast_to(two, (NB, NB)))[0:8].astype(jnp.int32)
    load_table = pltpu.make_async_copy(rows_v, table, local.at[5])
    load_table.start()
    bias = jnp.transpose(jnp.broadcast_to(jnp.concatenate([bias_ref[...], bias_ref[...]], axis=1), (2 * HD, 2 * HD)))[0:HD]
    bias = jnp.concatenate([bias, bias], axis=1)

    load_feat.wait()
    own = core * HALF + z * GROUP + y * NX + x
    X[own, 0] = feat_in[:, 0:TILE]
    X[own, 1] = feat_in[:, TILE:]
    pl.semaphore_wait(barrier, 18)

    gathered_all = gather_blocks(X, me, sy.at[0], ry.at[0], sR, rR, sL, rL, sXR, rXR, sXL, rXL, sP, rP)

    load_weight.wait()
    zero_th = to_feat(WR, f, sf.at[0], rf.at[0])
    load_near.wait()
    load_far.wait()
    total = jnp.zeros((HD, ROWS), F32)
    for s in range(BAND):
        spot = spot_of(rem(b + NB + s - 3, NB))
        total += dot(jnp.concatenate([X[spot, 0], X[spot, 1]], axis=1), near[s], NT)

    def far_forward(n, sums):
        low, high = sums
        for r in range(8):
            q = n * 8 + r
            value = dot(X[within(spot_of(source_ref[0, q]), NB - 1), within(index_ref[1, q], 1)], far[q], NT)
            first = index_ref[0, q] == 0
            low += jnp.where(first, value, 0.0)
            high += jnp.where(first, 0.0, value)
        return low, high

    zero = jnp.zeros((HD, TILE), F32)
    low, high = lax.fori_loop(0, FAR // 8, far_forward, (zero, zero))
    A[f] = (total + jnp.concatenate([low, high], axis=1)).astype(BF16)
    first = to_feat(A, f, sf.at[1], rf.at[1])
    from_feat(WR, f, sf.at[0], rf.at[0])
    WT[...] = jnp.transpose(WR[...].reshape(NF * HD, NF * HD).astype(F32))
    load_gout.wait()
    from_feat(A, f, sf.at[1], rf.at[1])

    gathered = A[...].reshape(NF * HD, ROWS)
    pre = dot(WR[f], gathered, NN) + bias
    sig = jax.nn.sigmoid(pre)
    grad_pre = (gout_in[...].astype(F32) * sig * (1.0 + pre * (1.0 - sig))).astype(BF16)
    GP[f] = grad_pre
    second = to_feat(GP, f, sf.at[2], rf.at[2])
    part = dot(grad_pre, gathered, NT)
    ones = dot(jnp.ones((8, ROWS), BF16), grad_pre, NT)
    side = jnp.concatenate([ones, ones], axis=1)
    for k in range(2):
        W0[k, :, 0:8, :] = part[:, k * 128:k * 128 + 128].reshape(8, 8, 128)
        for n in range(8):
            W0[k, n, 8:16, :] = side
    halves = send(W0.at[1 - core], W1, sw.at[0], rw.at[0], blk=partner)
    halves.start()
    act_ref[...] = (pre * sig).astype(BF16)
    from_feat(GP, f, sf.at[2], rf.at[2])
    own_rows = WT[pl.ds(pl.multiple_of(f * HD, HD), HD), :].astype(BF16)
    grad = dot(own_rows, GP[...].reshape(NF * HD, ROWS), NN).astype(BF16)
    ga[0] = grad[:, 0:TILE]
    ga[1] = grad[:, TILE:]

    halves.wait_recv()
    W2[...] = W0[core] + W1[...]
    to_z = []
    for d in range(1, NZ):
        zz = rem(z + d, NZ)
        to_z.append(send(W2.at[zz], W3.at[d - 1], sz.at[d - 1], rz.at[d - 1], blk=at(x, zz, y, core)))
        to_z[-1].start()

    def far_backward(n, _):
        for r in range(8):
            q = n * 8 + r
            parts[q] = dot(ga[within(index_ref[0, q], 1)], far[q], NN).astype(BF16)
        return 0

    lax.fori_loop(0, FAR // 8, far_backward, 0)
    parts[FAR] = jnp.zeros((HD, TILE), BF16)
    for s in range(BAND):
        value = dot(grad, near[s], NN)
        band[s, 0] = value[:, 0:TILE]
        band[s, 1] = value[:, TILE:]

    to_slab, again = [], []
    for e in range(1, 8):
        xx, yy = slab(e)
        to_slab.append(send(W5.at[x * NY + y], W5.at[x * NY + y], sq.at[e - 1], rq.at[e - 1], blk=at(xx, z, yy, core)))
    for d in range(1, NZ):
        again.append(send(W7.at[z], W7.at[z], sz2.at[d - 1], rz2.at[d - 1], blk=at(x, rem(z + d, NZ), y, core)))
    final = send(W7, W8, sw.at[1], rw.at[1], blk=partner)

    def sum_z():
        for copy in to_z:
            copy.wait_recv()
        mine = W2[z]
        for d in range(NZ - 1):
            mine += W3[d]
        W5[x * NY + y] = mine
        for copy in to_slab:
            copy.start()

    def sum_slab():
        for e in range(1, 8):
            ref = W5.at[rem(x + NX - e // 2, NX) * NY + (y + e % 2) % 2]
            send(ref, ref, sq.at[e - 1], rq.at[e - 1], blk=partner).wait_recv()
        total = W5[0]
        for n in range(1, 8):
            total += W5[n]
        W7[z] = total
        for copy in again:
            copy.start()

    def spread_z():
        for d in range(1, NZ):
            ref = W7.at[rem(z + NZ - d, NZ)]
            send(ref, ref, sz2.at[d - 1], rz2.at[d - 1], blk=partner).wait_recv()
        final.start()

    sum_z()
    hooks = {6: sum_slab, 14: spread_z}
    given, run, sent = scatter_blocks(
        G, H, XE, XW, RR, RL, Fs, Fr, gfeat_ref, me, hooks,
        sH, rH, tXR, uXR, tXL, uXL, tR, uR, tL, uL, sy.at[1], ry.at[1],
    )

    def place(c):
        one, two = table[0, c], table[8, c]
        va, vb = parts[within(one // 2, FAR)].astype(F32), parts[within(two // 2, FAR)].astype(F32)
        ua, ub = one % 2 == 0, two % 2 == 0
        G[c, 0] = (jnp.where(ua, va, 0.0) + jnp.where(ub, vb, 0.0)).astype(BF16)
        G[c, 1] = (jnp.where(ua, 0.0, va) + jnp.where(ub, 0.0, vb)).astype(BF16)

    def group(j, w):
        return rem(z + 4 + j // 2 + (j % 2) * (NZ - j), NZ), (1 - y, y)[w]

    def fill(j, w):
        zz, yy = group(j, w)
        for k in (1 - core, core):
            for r in range(NX):
                place(k * HALF + zz * GROUP + yy * NX + r)

    def give(j, w):
        zz, yy = group(j, w)
        given(zz, yy, j * 2 + w).start()

    def fill_and_give(w, j, _):
        fill(j, w)
        give(j, w)
        return 0

    def fill_near(j, _):
        fill(j, 0)
        fill(j, 1)
        return 0

    load_table.wait()
    lax.fori_loop(0, 5, functools.partial(fill_and_give, 0), 0)
    lax.fori_loop(5, 8, fill_near, 0)
    for s in range(BAND):
        spot = spot_of(rem(b + NB + s - 3, NB))
        G[spot] = (G[spot].astype(F32) + band[s]).astype(BF16)
    for j in (5, 6, 7):
        give(j, 0)
    lax.fori_loop(0, 5, functools.partial(fill_and_give, 1), 0)
    for j in (5, 6, 7):
        give(j, 1)

    run()
    final.wait_recv()
    for k in range(2):
        value = jnp.where(core == k, W7[...], W8[...])
        gw_ref[:, k * 128:k * 128 + 128] = value[:, 0:8, :].reshape(HD, 128)
    gb_ref[...] = jnp.where(core == 0, W7[0, 8:9, :], W8[0, 8:9, :])[:, 0:HD]

    gathered_all()
    sent()
    halves.wait_send()
    for copy in zero_th + first + second + to_z + to_slab + again + [final]:
        copy.wait_send()


def on_device(features, near_tiles, far_tiles, far_source, far_index, weight, bias, grad_out):
    near = jnp.transpose(near_tiles, (1, 0, 2))
    source, index = far_source.T, far_index.T
    vmem, smem, any_ = (pl.BlockSpec(memory_space=s) for s in (pltpu.VMEM, pltpu.SMEM, pl.ANY))
    dma = lambda *shape: pltpu.SemaphoreType.DMA(shape)
    one = pltpu.SemaphoreType.DMA
    block = (2, HD, TILE)
    act, gfeat, gw, gb = pl.pallas_call(
        kernel,
        out_shape=(
            jax.ShapeDtypeStruct((HD, ROWS), BF16),
            jax.ShapeDtypeStruct((HD, ROWS), BF16),
            jax.ShapeDtypeStruct((HD, NF * HD), F32),
            jax.ShapeDtypeStruct((1, HD), F32),
        ),
        in_specs=[any_, any_, any_, smem, smem, vmem, vmem, any_, vmem, any_],
        out_specs=(vmem,) * 4,
        scratch_shapes=[
            pltpu.VMEM((BAND, ROWS, ROWS), BF16),
            pltpu.VMEM((FAR, TILE, TILE), BF16),
            pltpu.VMEM((HD, ROWS), BF16),
            pltpu.VMEM((HD, ROWS), BF16),
            pltpu.VMEM((NB,) + block, BF16),
            pltpu.VMEM((NB,) + block, BF16),
            pltpu.VMEM((HALF,) + block, BF16),
            pltpu.VMEM((16, 2) + block, BF16),
            pltpu.VMEM((16, 2) + block, BF16),
            pltpu.VMEM((2, 4, NX) + block, BF16),
            pltpu.VMEM((2, 4, NX) + block, BF16),
            pltpu.VMEM((NY,) + block, BF16),
            pltpu.VMEM(block, BF16),
            pltpu.VMEM((NF, HD, ROWS), BF16),
            pltpu.VMEM((NF, HD, ROWS), BF16),
            pltpu.VMEM((NF, HD, ROWS), BF16),
            pltpu.VMEM((NF * HD, NF * HD), F32),
            pltpu.VMEM(block, BF16),
            pltpu.VMEM((FAR + 1, HD, TILE), BF16),
            pltpu.VMEM((BAND,) + block, F32),
            pltpu.VMEM((16, NB), jnp.int32),
            pltpu.SMEM((16, NB), jnp.int32),
            pltpu.VMEM((2, 8, 16, 128), F32),
            pltpu.VMEM((8, 16, 128), F32),
            pltpu.VMEM((8, 16, 128), F32),
            pltpu.VMEM((7, 16, 128), F32),
            pltpu.VMEM((8, 16, 128), F32),
            pltpu.VMEM((8, 16, 128), F32),
            pltpu.VMEM((8, 16, 128), F32),
            dma(6), dma(2), dma(2),
            dma(2, 4, 4), dma(2, 4, 4), dma(2, 4, 4), dma(2, 4, 4),
            dma(2, 8, 2), dma(2, 8, 2), dma(2, 8, 2), dma(2, 8, 2), one, one,
            dma(3, 3), dma(3, 3), dma(16), dma(16),
            dma(16, 2), dma(16, 2), dma(16, 2), dma(16, 2),
            dma(2, 4, 4), dma(2, 4, 4), dma(2, 4, 4), dma(2, 4, 4),
            dma(2), dma(2), dma(7), dma(7), dma(7), dma(7), dma(7), dma(7),
        ],
        compiler_params=pltpu.CompilerParams(
            collective_id=0, has_side_effects=True, vmem_limit_bytes=60 * 2**20
        ),
    )(features, near, far_tiles, source, index, source, index, weight.T, bias[None, :], grad_out)
    return act, gfeat, gw.T, gb[0]


def solution(mesh):
    return jax.shard_map(
        on_device,
        mesh=mesh,
        in_specs=(
            P("feat", "blk"),
            P("blk", None, None),
            P("blk", None, None),
            P("blk", None),
            P("blk", None),
            P(None, "feat"),
            P("feat"),
            P("feat", "blk"),
        ),
        out_specs=(P("feat", "blk"), P("feat", "blk"), P(None, "feat"), P("feat")),
        check_vma=False,
    )
```

```python
import functools

import jax
import jax.numpy as jnp
from jax import lax
from jax.experimental import pallas as pl
from jax.experimental.pallas import tpu as pltpu
from jax.sharding import PartitionSpec as P

NX, NZ, NY, NC = 4, 8, 2, 2
NB = NX * NZ * NY * NC
HALF = NB // NC
GROUP = NX * NY
FAR = 96
BAND = 7
NF = 4
HD = 64
TILE = 128
ROWS = 256
F32 = jnp.float32
BF16 = jnp.bfloat16
NN = (((1,), (0,)), ((), ()))
NT = (((1,), (1,)), ((), ()))
TN = (((0,), (0,)), ((), ()))
STEPS = (4, 3, -3, 2, -2, 1, -1, 0)


def dot(a, b, dims):
    return lax.dot_general(a, b, dims, preferred_element_type=F32)


def send(src, dst, sent, got, **where):
    return pltpu.make_async_remote_copy(
        src_ref=src, dst_ref=dst, send_sem=sent, recv_sem=got,
        device_id=where, device_id_type=pl.DeviceIdType.MESH,
    )


def rem(a, n):
    return lax.rem(a, jnp.int32(n))


def within(n, most):
    return jnp.minimum(jnp.maximum(n, 0), most)


def spot_of(c):
    return (c % 2) * HALF + ((c // 4) % 8) * GROUP + ((c // 2) % 2) * NX + c // 32


def gather_blocks(X, me, share, sy, ry, sR, rR, sL, rL, sXR, rXR, sXL, rXL, sP, rP):
    x, z, y, core, at = me
    east, west = at(rem(x + 1, NX), z, y, core), at(rem(x + NX - 1, NX), z, y, core)
    partner, across = at(x, z, y, 1 - core), at(x, z, 1 - y, core)
    ys = (y, 1 - y)

    def block(k, xx, zz, w):
        return k * HALF + zz * GROUP + ys[w] * NX + xx

    def whole(k, xx, zz, w):
        return X.at[block(k, xx, zz, w)]

    swap = send(whole(core, x, z, 0), whole(core, x, z, 0), sy, ry, blk=across)
    swap.start()

    def swapped():
        send(whole(core, x, z, 1), whole(core, x, z, 1), sy, ry, blk=across).wait_recv()

    def hand(k, zz, w, wait=False):
        ref = X.at[pl.ds(k * HALF + zz * GROUP + ys[w] * NX, NX)]
        copy = send(ref, ref, sP, rP, blk=partner)
        copy.start()

    def ring_parts(k, xx, i, w, wide):
        out = []
        for sign, ss, rr in ((1, sR, rR), (-1, sL, rL)):
            def step(n, zd, hops, half, ss=ss, rr=rr, sign=sign):
                src = whole(k, xx, rem(z + NZ - sign * zd, NZ), w)
                src = src if half is None else src.at[half]
                return send(src, src, ss.at[w, i, n], rr.at[w, i, n], blk=at(x, rem(z + NZ + sign * hops, NZ), y, core))

            half = 0 if sign == 1 else 1
            out.append((
                functools.partial(step, 0, 0, 1, None),
                functools.partial(step, 1, 0, 2, None) if wide else functools.partial(step, 1, 1, 1, None),
                functools.partial(step, 2, 2, 1, None),
                functools.partial(step, 3, 2, 2, half),
            ))
        return out

    def ring_got(k, xx, i, w, n):
        for sign, ss, rr, u in ((1, sR, rR, 0), (-1, sL, rL, 1)):
            ref = whole(k, xx, rem(z + NZ - sign * (n + 1), NZ), w)
            ref = ref if n < 3 else ref.at[u]
            send(ref, ref, ss.at[w, i, n], rr.at[w, i, n], blk=partner).wait_recv()

    def ring_start(k, xx, i, w, wide):
        parts = ring_parts(k, xx, i, w, wide)
        if wide:
            parts[0][1]().start()
            parts[1][1]().start()
        parts[0][0]().start()
        parts[1][0]().start()

    def ring_second(k, xx, i, w):
        ring_got(k, xx, i, w, 0)
        for part in ring_parts(k, xx, i, w, False):
            part[1]().start()

    def ring_third(k, xx, i, w):
        ring_got(k, xx, i, w, 1)
        for part in ring_parts(k, xx, i, w, True):
            part[3]().start()
            part[2]().start()

    def ring_sent(k, xx, i, w, wide):
        for part in ring_parts(k, xx, i, w, wide):
            for copy in part:
                copy().wait_send()

    def x_step(k, zz, j, w, s, what):
        for xx, ss, rr, to, u in ((rem(x + NX - s, NX), sXR, rXR, east, 0), (rem(x + s, NX), sXL, rXL, west, 1)):
            ref = whole(k, xx, zz, w)
            if what == "go" and s > 0:
                got = ref if s < 2 else ref.at[u]
                send(got, got, ss.at[w, j, s - 1], rr.at[w, j, s - 1], blk=to).wait_recv()
            if s < 2:
                out = ref if s < 1 else ref.at[u]
                copy = send(out, out, ss.at[w, j, s], rr.at[w, j, s], blk=to)
                copy.start() if what == "go" else copy.wait_send()

    def places(s):
        if s == 0:
            return [(z, 0)]
        if s == 4:
            return [(rem(z + 4, NZ), 7)]
        return [(rem(z + NZ - s, NZ), 2 * s - 1), (rem(z + s, NZ), 2 * s)]

    def across_x(w):
        ref = whole(1, x, z, w)
        return (
            send(ref, ref, sXR.at[w, 0, 0], rXR.at[w, 0, 0], blk=east),
            send(ref, ref, sXL.at[w, 0, 0], rXL.at[w, 0, 0], blk=west),
            send(ref, ref, sXR.at[w, 0, 1], rXR.at[w, 0, 1], blk=at(rem(x + 2, NX), z, y, core)),
        )

    def from_x(w, i):
        ref = whole(1, rem(x + NX - i, NX), z, w)
        ss, rr, n = ((sXR, rXR, 0), (sXR, rXR, 1), (sXL, rXL, 0))[i - 1]
        send(ref, ref, ss.at[w, 0, n], rr.at[w, 0, n], blk=partner).wait_recv()

    def hop(s, w, n):
        for zz, j in places(s):
            x_step(0, zz, j, w, n, "go")
            if n == 2:
                hand(0, zz, w)

    @pl.when(core == 0)
    def _():
        def got(n, w):
            ring_got(0, x, 0, w, n)
            hop(n + 1, w, 0)

        def third(w):
            ring_third(0, x, 0, w)
            hop(2, w, 0)

        ring_start(0, x, 0, 0, True)
        hop(0, 0, 0)
        third(0)
        got(0, 0)
        swapped()
        ring_start(0, x, 0, 1, True)
        share()
        hop(0, 1, 0)
        hop(0, 0, 1)
        got(2, 0)
        got(3, 0)
        hop(2, 0, 1)
        hop(1, 0, 1)
        hop(0, 0, 2)
        third(1)
        got(0, 1)
        for s, w, n in ((0, 1, 1), (3, 0, 1), (4, 0, 1), (2, 0, 2), (1, 0, 2)):
            hop(s, w, n)
        got(2, 1)
        got(3, 1)
        for s, w, n in (
            (2, 1, 1), (1, 1, 1), (3, 0, 2), (4, 0, 2), (0, 1, 2), (3, 1, 1), (4, 1, 1),
            (2, 1, 2), (1, 1, 2), (3, 1, 2), (4, 1, 2),
        ):
            hop(s, w, n)

    @pl.when(core == 1)
    def _():
        every = (0, 1, 3, 2)

        def xs(i):
            return rem(x + NX - i, NX)

        def spread(w):
            for i in (1, 3, 2):
                from_x(w, i)
                ring_start(1, xs(i), i, w, False)
            hand(1, z, w)

        def second(w, which):
            for i in which:
                ring_second(1, xs(i), i, w)

        def third(w, which):
            for i in which:
                ring_third(1, xs(i), i, w)

        def done(w, n):
            for i in every:
                ring_got(1, xs(i), i, w, n)
            for zz, j in places(n + 1):
                hand(1, zz, w)

        def along(w, n):
            for zz, j in places(n + 1):
                hand(1, zz, w)

        for copy in across_x(0):
            copy.start()
        ring_start(1, x, 0, 0, False)
        spread(0)
        second(0, (0,))
        swapped()
        for copy in across_x(1):
            copy.start()
        ring_start(1, x, 0, 1, False)
        share()
        second(0, (1, 3, 2))
        along(0, 0)
        third(0, (0,))
        spread(1)
        second(1, (0,))
        third(0, (1, 3, 2))
        along(0, 1)
        second(1, (1, 3, 2))
        along(1, 0)
        third(1, (0,))
        done(0, 2)
        done(0, 3)
        third(1, (1, 3, 2))
        along(1, 1)
        done(1, 2)
        done(1, 3)

    theirs = X.at[pl.ds((1 - core) * HALF, HALF)]
    send(theirs, theirs, sP, rP, blk=partner).wait_recv()

    def finish():
        swap.wait_send()
        ours = X.at[pl.ds(core * HALF, HALF)]
        send(ours, ours, sP, rP, blk=partner).wait_send()

        @pl.when(core == 0)
        def _():
            for w in (0, 1):
                ring_sent(0, x, 0, w, True)
                for s in range(5):
                    for zz, j in places(s):
                        x_step(0, zz, j, w, 0, "end")
                        x_step(0, zz, j, w, 1, "end")

        @pl.when(core == 1)
        def _():
            for w in (0, 1):
                for copy in across_x(w):
                    copy.wait_send()
                for i in range(4):
                    ring_sent(1, rem(x + NX - i, NX), i, w, False)

    return finish


def to_feat(S, f, sent, got):
    return [send(S.at[f], S.at[f], sent.at[d - 1], got.at[d - 1], feat=rem(f + d, NF)) for d in (1, 2, 3)]


def from_feat(S, f, sent, got):
    for d in (1, 2, 3):
        ref = S.at[rem(f + NF - d, NF)]
        send(ref, ref, sent.at[d - 1], got.at[d - 1], feat=rem(f + d, NF)).wait_recv()


def add_to(G, at, u, *more):
    if u is None:
        total = G[at].astype(F32)
        for m in more:
            total += m.astype(F32)
        G[at] = total.astype(BF16)
    else:
        total = G[at, u].astype(F32)
        for m in more:
            total += m.astype(F32)
        G[at, u] = total.astype(BF16)


def scatter_blocks(G, H, XE, XW, RR, RL, Fs, Fr, out, me, hooks, sH, rH, sXR, rXR, sXL, rXL, sR, rR, sL, rL, sy, ry):
    x, z, y, core, at = me
    east, west = at(rem(x + 1, NX), z, y, core), at(rem(x + NX - 1, NX), z, y, core)
    partner, across = at(x, z, y, 1 - core), at(x, z, 1 - y, core)
    zs = [rem(z + o + NZ, NZ) for o in STEPS]
    ys = (1 - y, y)
    mine, theirs = core * HALF, (1 - core) * HALF

    def block(xx, j, w):
        return mine + zs[j] * GROUP + ys[w] * NX + xx

    def given(zz, yy, n):
        ref = G.at[pl.ds(theirs + zz * GROUP + yy * NX, NX)]
        return send(ref, H.at[pl.ds(zz * GROUP + yy * NX, NX)], sH.at[n], rH.at[n], blk=partner)

    def taken(j, w):
        base = zs[j] * GROUP + ys[w] * NX
        ref = H.at[pl.ds(base, NX)]
        send(ref, ref, sH.at[j * 2 + w], rH.at[j * 2 + w], blk=partner).wait_recv()
        for n in range(NX):
            add_to(G, mine + base + n, None, H[base + n])

    def ring_copy(xx, i, w, n, way, wide):
        R, ss, rr, sign = (RR, sR, rR, 1) if way == 0 else (RL, sL, rL, -1)
        src = G.at[mine + rem(z + NZ + sign * (n + 1), NZ) * GROUP + ys[w] * NX + xx]
        dst = R.at[w, n, i]
        if n == 3:
            src, dst = src.at[way], dst.at[way]
        hops = 2 if n == 3 or (n == 1 and wide) else 1
        return send(src, dst, ss.at[w, i, n], rr.at[w, i, n], blk=at(x, rem(z + NZ + sign * hops, NZ), y, core))

    def ring_wait(i, w, n, way):
        R, ss, rr = (RR, sR, rR) if way == 0 else (RL, sL, rL)
        ref = R.at[w, n, i, way] if n == 3 else R.at[w, n, i]
        send(ref, ref, ss.at[w, i, n], rr.at[w, i, n], blk=partner).wait_recv()

    def ring(xx, i, j, w, wide):
        if j == 0:
            for way in (0, 1):
                ring_copy(xx, i, w, 3, way, wide).start()
            return
        if j == 7:
            total = G[block(xx, 7, w)].astype(F32)
            for way, R in ((0, RR), (1, RL)):
                for n in (0, 1) if wide else (0,):
                    ring_wait(i, w, n, way)
                    total += R[w, n, i].astype(F32)
            return total
        way, n = (j + 1) % 2, 2 - (j - 1) // 2
        R, base = (RR, RL)[way], block(xx, j, w)
        if n == 1:
            ring_wait(i, w, 3, way)
            ring_wait(i, w, 2, way)
            add_to(G, base, way, R[w, 3, i, way])
            add_to(G, base, None, R[w, 2, i])
        if n == 0 and not wide:
            ring_wait(i, w, 1, way)
            add_to(G, base, None, R[w, 1, i])
        ring_copy(xx, i, w, n, way, wide).start()

    def ring_sent(xx, i, w, wide):
        for n in range(4):
            for way in (0, 1):
                ring_copy(xx, i, w, n, way, wide).wait_send()

    def x_copies(j, w, s):
        far, near_e, near_w = block(rem(x + 2, NX), j, w), block(rem(x + 1, NX), j, w), block(rem(x + NX - 1, NX), j, w)
        n = j * 2 + w
        if s == 0:
            return (send(G.at[far, 0], XE.at[n, 0, 0], sXR.at[n, 0], rXR.at[n, 0], blk=east),
                    send(G.at[far, 1], XW.at[n, 0, 1], sXL.at[n, 0], rXL.at[n, 0], blk=west))
        return (send(G.at[near_e], XE.at[n, 1], sXR.at[n, 1], rXR.at[n, 1], blk=east),
                send(G.at[near_w], XW.at[n, 1], sXL.at[n, 1], rXL.at[n, 1], blk=west))

    def x_step(j, w, s):
        n = j * 2 + w
        if s > 0:
            for copy in x_copies(j, w, s - 1):
                copy.wait_recv()
        if s == 1:
            add_to(G, block(rem(x + 1, NX), j, w), 0, XE[n, 0, 0])
            add_to(G, block(rem(x + NX - 1, NX), j, w), 1, XW[n, 0, 1])
        if s < 2:
            for copy in x_copies(j, w, s):
                copy.start()

    def x_total(j, w):
        n = j * 2 + w
        return G[block(x, j, w)].astype(F32) + XE[n, 1].astype(F32) + XW[n, 1].astype(F32)

    def across_x(w):
        n = 14 + w
        return (
            send(G.at[block(rem(x + 1, NX), 7, w)], XE.at[n, 1], sXR.at[n, 1], rXR.at[n, 1], blk=east),
            send(G.at[block(rem(x + NX - 1, NX), 7, w)], XW.at[n, 1], sXL.at[n, 1], rXL.at[n, 1], blk=west),
            send(G.at[block(rem(x + 2, NX), 7, w)], XE.at[n, 0], sXR.at[n, 0], rXR.at[n, 0], blk=at(rem(x + 2, NX), z, y, core)),
        )

    def from_x(w):
        for copy in across_x(w):
            copy.wait_recv()
        return x_total(7, w) + XE[14 + w, 0].astype(F32)

    order = tuple((j, w) for j in range(8) for w in range(2))
    last = send(Fs.at[0], Fr, sy, ry, blk=across)

    def deliver(w, total):
        Fs[w] = total.astype(BF16)
        if w == 0:
            last.start()

    def run():
        @pl.when(core == 0)
        def _():
            for n in range(len(order) + 8):
                if n < len(order):
                    taken(*order[n])
                    x_step(*order[n], 0)
                if 0 <= n - 4 < len(order):
                    x_step(*order[n - 4], 1)
                if 0 <= n - 8:
                    j, w = order[n - 8]
                    x_step(j, w, 2)
                    G[block(x, j, w)] = x_total(j, w).astype(BF16)
                    total = ring(x, 0, j, w, True)
                    if j == 7:
                        deliver(w, total)
                if n in hooks:
                    hooks[n]()

        @pl.when(core == 1)
        def _():
            for n, (j, w) in enumerate(order):
                taken(j, w)
                for i in (2, 1, 3, 0):
                    xx = rem(x + i, NX)
                    total = ring(xx, i, j, w, False)
                    if j == 7:
                        G[block(xx, 7, w)] = total.astype(BF16)
                if j == 7:
                    for copy in across_x(w):
                        copy.start()
                if (j, w) == (7, 1):
                    deliver(0, from_x(0))
                    deliver(1, from_x(1))
                if n in hooks:
                    hooks[n]()

        last.wait_recv()
        total = Fs[1].astype(F32) + Fr[...].astype(F32)
        out[:, 0:TILE] = total[0].astype(BF16)
        out[:, TILE:] = total[1].astype(BF16)

    def finish():
        last.wait_send()
        for j in range(8):
            for w in range(2):
                given(zs[j], ys[w], j * 2 + w).wait_send()

        @pl.when(core == 0)
        def _():
            for w in range(2):
                ring_sent(x, 0, w, True)
                for j in range(8):
                    for s in range(2):
                        for copy in x_copies(j, w, s):
                            copy.wait_send()

        @pl.when(core == 1)
        def _():
            for w in range(2):
                for i in range(4):
                    ring_sent(rem(x + i, NX), i, w, False)
                for copy in across_x(w):
                    copy.wait_send()

    return given, run, finish


def kernel(
    feat_hbm, near_hbm, far_hbm, source_ref, index_ref, source_row, index_row, weight_hbm, bias_ref, gout_hbm,
    act_ref, gfeat_ref, gw_ref, gb_ref,
    near, far, feat_in, X, G, H, XE, XW, RR, RL, Fs, Fr, A, GP, WR, WT, GO, BI, BC, ga, parts, band, rows_v, table,
    W0, W1, W2, W3, W5, W7, W8,
    local, sy, ry, sR, rR, sL, rL, sXR, rXR, sXL, rXL, sP, rP,
    sf, rf, sH, rH, tXR, uXR, tXL, uXL, tR, uR, tL, uL, sw, rw, sz, rz, sq, rq, sz2, rz2,
):
    b, f = lax.axis_index("blk"), lax.axis_index("feat")
    core, y, z, x = b % 2, (b // 2) % 2, (b // 4) % 8, b // 32

    def at(xx, zz, yy, cc):
        return ((xx * NZ + zz) * NY + yy) * NC + cc

    me = (x, z, y, core, at)
    partner = at(x, z, y, 1 - core)

    def slab(e):
        return rem(x + e // 2, NX), (y + e % 2) % 2

    def signal(**where):
        pl.semaphore_signal(barrier, 1, device_id=where, device_id_type=pl.DeviceIdType.MESH)

    barrier = pltpu.get_barrier_semaphore()
    signal(blk=partner)
    for e in range(1, 8):
        xx, yy = slab(e)
        signal(blk=at(xx, z, yy, core))
    for d in range(1, NZ):
        signal(blk=at(x, rem(z + d, NZ), y, core))
    for d in (1, 2, 3):
        signal(feat=rem(f + d, NF))

    load_feat = pltpu.make_async_copy(feat_hbm, feat_in, local.at[0])
    load_weight = pltpu.make_async_copy(weight_hbm, WR.at[f], local.at[1])
    load_gout = pltpu.make_async_copy(gout_hbm, GO.at[f], local.at[2])
    load_near = pltpu.make_async_copy(near_hbm, near, local.at[3])
    load_far = pltpu.make_async_copy(far_hbm, far, local.at[4])
    for load in (load_feat, load_weight, load_gout, load_near, load_far):
        load.start()

    BI[f] = jnp.broadcast_to(jnp.concatenate([bias_ref[...], bias_ref[...]], axis=1), (8, 2 * HD))
    load_feat.wait()
    own = core * HALF + z * GROUP + y * NX + x
    X[own, 0] = feat_in[:, 0:TILE]
    X[own, 1] = feat_in[:, TILE:]
    pl.semaphore_wait(barrier, 18)

    load_weight.wait()
    load_gout.wait()

    def share():
        for n, S in ((0, WR), (2, GO), (3, BI)):
            for copy in to_feat(S, f, sf.at[n], rf.at[n]):
                copy.start()

    gathered_all = gather_blocks(X, me, share, sy.at[0], ry.at[0], sR, rR, sL, rL, sXR, rXR, sXL, rXL, sP, rP)

    load_near.wait()
    load_far.wait()
    total = jnp.zeros((HD, ROWS), F32)
    for s in range(BAND):
        spot = spot_of(rem(b + NB + s - 3, NB))
        total += dot(jnp.concatenate([X[spot, 0], X[spot, 1]], axis=1), near[s], NT)

    def far_forward(n, sums):
        low, high = sums
        for r in range(8):
            q = n * 8 + r
            value = dot(X[within(spot_of(source_ref[0, q]), NB - 1), within(index_ref[1, q], 1)], far[q], NT)
            first = index_ref[0, q] == 0
            low += jnp.where(first, value, 0.0)
            high += jnp.where(first, 0.0, value)
        return low, high

    zero = jnp.zeros((HD, TILE), F32)
    low, high = lax.fori_loop(0, FAR // 8, far_forward, (zero, zero))
    A[f] = (total + jnp.concatenate([low, high], axis=1)).astype(BF16)
    for copy in to_feat(A, f, sf.at[1], rf.at[1]):
        copy.start()
    for n, S in ((0, WR), (2, GO), (3, BI)):
        from_feat(S, f, sf.at[n], rf.at[n])
    WT[...] = jnp.transpose(WR[...].reshape(NF * HD, NF * HD).astype(F32))
    for n in range(NF):
        column = jnp.transpose(jnp.broadcast_to(BI[n, 0:1, :], (2 * HD, 2 * HD)))[0:HD]
        BC[n, :, 0:TILE] = column
        BC[n, :, TILE:] = column

    places = jnp.broadcast_to(spot_of(source_row[...]), (NB, FAR))
    keys = jnp.broadcast_to((lax.broadcasted_iota(jnp.int32, (1, FAR), 1) * 2 + index_row[1:2, :]).astype(F32), (NB, FAR))
    match = places == lax.broadcasted_iota(jnp.int32, (NB, FAR), 0)
    one = jnp.min(jnp.where(match, keys, 2.0 * FAR), axis=1, keepdims=True)
    two = jnp.max(jnp.where(match, keys, -1.0), axis=1, keepdims=True)
    two = jnp.where((two == one) | (two < 0.0), 2.0 * FAR, two)
    rows_v[0:8] = jnp.transpose(jnp.broadcast_to(one, (NB, NB)))[0:8].astype(jnp.int32)
    rows_v[8:16] = jnp.transpose(jnp.broadcast_to(two, (NB, NB)))[0:8].astype(jnp.int32)
    load_table = pltpu.make_async_copy(rows_v, table, local.at[5])
    load_table.start()
    from_feat(A, f, sf.at[1], rf.at[1])

    gathered = A[...].reshape(NF * HD, ROWS)
    pre = dot(WR[...].reshape(NF * HD, NF * HD), gathered, NN) + BC[...].reshape(NF * HD, ROWS)
    sig = jax.nn.sigmoid(pre)
    upstream = GO[...].reshape(NF * HD, ROWS).astype(F32)
    every_grad_pre = (upstream * sig * (1.0 + pre * (1.0 - sig))).astype(BF16)
    GP[...] = every_grad_pre.reshape(NF, HD, ROWS)
    grad_pre = GP[f]
    part = dot(grad_pre, gathered, NT)
    ones = dot(jnp.ones((8, ROWS), BF16), grad_pre, NT)
    side = jnp.concatenate([ones, ones], axis=1)
    for k in range(2):
        W0[k, :, 0:8, :] = part[:, k * 128:k * 128 + 128].reshape(8, 8, 128)
        for n in range(8):
            W0[k, n, 8:16, :] = side
    halves = send(W0.at[1 - core], W1, sw.at[0], rw.at[0], blk=partner)
    halves.start()
    own_rows = WT[pl.ds(pl.multiple_of(f * HD, HD), HD), :].astype(BF16)
    grad = dot(own_rows, every_grad_pre, NN).astype(BF16)
    ga[0] = grad[:, 0:TILE]
    ga[1] = grad[:, TILE:]
    pre = dot(WR[f], gathered, NN) + BC[f]
    act_ref[...] = jax.nn.silu(pre).astype(BF16)

    halves.wait_recv()
    W2[...] = W0[core] + W1[...]
    to_z = []
    for d in range(1, NZ):
        zz = rem(z + d, NZ)
        to_z.append(send(W2.at[zz], W3.at[d - 1], sz.at[d - 1], rz.at[d - 1], blk=at(x, zz, y, core)))
        to_z[-1].start()

    def far_backward(n, _):
        for r in range(8):
            q = n * 8 + r
            parts[q] = dot(ga[within(index_ref[0, q], 1)], far[q], NN).astype(BF16)
        return 0

    lax.fori_loop(0, FAR // 8, far_backward, 0)
    parts[FAR] = jnp.zeros((HD, TILE), BF16)
    for s in range(BAND):
        value = dot(grad, near[s], NN)
        band[s, 0] = value[:, 0:TILE]
        band[s, 1] = value[:, TILE:]

    to_slab, again = [], []
    for e in range(1, 8):
        xx, yy = slab(e)
        to_slab.append(send(W5.at[x * NY + y], W5.at[x * NY + y], sq.at[e - 1], rq.at[e - 1], blk=at(xx, z, yy, core)))
    for d in range(1, NZ):
        again.append(send(W7.at[z], W7.at[z], sz2.at[d - 1], rz2.at[d - 1], blk=at(x, rem(z + d, NZ), y, core)))
    final = send(W7, W8, sw.at[1], rw.at[1], blk=partner)

    def sum_z():
        for copy in to_z:
            copy.wait_recv()
        mine = W2[z]
        for d in range(NZ - 1):
            mine += W3[d]
        W5[x * NY + y] = mine
        for copy in to_slab:
            copy.start()

    def sum_slab():
        for e in range(1, 8):
            ref = W5.at[rem(x + NX - e // 2, NX) * NY + (y + e % 2) % 2]
            send(ref, ref, sq.at[e - 1], rq.at[e - 1], blk=partner).wait_recv()
        total = W5[0]
        for n in range(1, 8):
            total += W5[n]
        W7[z] = total
        for copy in again:
            copy.start()

    def spread_z():
        for d in range(1, NZ):
            ref = W7.at[rem(z + NZ - d, NZ)]
            send(ref, ref, sz2.at[d - 1], rz2.at[d - 1], blk=partner).wait_recv()
        final.start()

    sum_z()
    hooks = {6: sum_slab, 14: spread_z}
    given, run, sent = scatter_blocks(
        G, H, XE, XW, RR, RL, Fs, Fr, gfeat_ref, me, hooks,
        sH, rH, tXR, uXR, tXL, uXL, tR, uR, tL, uL, sy.at[1], ry.at[1],
    )

    def place(c):
        one, two = table[0, c], table[8, c]
        va, vb = parts[within(one // 2, FAR)].astype(F32), parts[within(two // 2, FAR)].astype(F32)
        ua, ub = one % 2 == 0, two % 2 == 0
        G[c, 0] = (jnp.where(ua, va, 0.0) + jnp.where(ub, vb, 0.0)).astype(BF16)
        G[c, 1] = (jnp.where(ua, 0.0, va) + jnp.where(ub, 0.0, vb)).astype(BF16)

    def group(j, w):
        return rem(z + 4 + j // 2 + (j % 2) * (NZ - j), NZ), (1 - y, y)[w]

    def fill(j, w):
        zz, yy = group(j, w)
        for k in (1 - core, core):
            for r in range(NX):
                place(k * HALF + zz * GROUP + yy * NX + r)

    def give(j, w):
        zz, yy = group(j, w)
        given(zz, yy, j * 2 + w).start()

    def fill_and_give(j, _):
        for w in (0, 1):
            fill(j, w)
            give(j, w)
        return 0

    def fill_near(j, _):
        fill(j, 0)
        fill(j, 1)
        return 0

    load_table.wait()
    lax.fori_loop(0, 5, fill_and_give, 0)
    lax.fori_loop(5, 8, fill_near, 0)
    for s in range(BAND):
        spot = spot_of(rem(b + NB + s - 3, NB))
        G[spot] = (G[spot].astype(F32) + band[s]).astype(BF16)
    for j in (5, 6, 7):
        give(j, 0)
        give(j, 1)

    run()
    final.wait_recv()
    for k in range(2):
        value = jnp.where(core == k, W7[...], W8[...])
        gw_ref[:, k * 128:k * 128 + 128] = value[:, 0:8, :].reshape(HD, 128)
    gb_ref[...] = jnp.where(core == 0, W7[0, 8:9, :], W8[0, 8:9, :])[:, 0:HD]

    gathered_all()
    sent()
    halves.wait_send()
    for n, S in enumerate((WR, A, GO, BI)):
        for copy in to_feat(S, f, sf.at[n], rf.at[n]):
            copy.wait_send()
    for copy in to_z + to_slab + again + [final]:
        copy.wait_send()


def on_device(features, near_tiles, far_tiles, far_source, far_index, weight, bias, grad_out):
    near = jnp.transpose(near_tiles, (1, 0, 2))
    source, index = far_source.T, far_index.T
    vmem, smem, any_ = (pl.BlockSpec(memory_space=s) for s in (pltpu.VMEM, pltpu.SMEM, pl.ANY))
    dma = lambda *shape: pltpu.SemaphoreType.DMA(shape)
    one = pltpu.SemaphoreType.DMA
    block = (2, HD, TILE)
    act, gfeat, gw, gb = pl.pallas_call(
        kernel,
        out_shape=(
            jax.ShapeDtypeStruct((HD, ROWS), BF16),
            jax.ShapeDtypeStruct((HD, ROWS), BF16),
            jax.ShapeDtypeStruct((HD, NF * HD), F32),
            jax.ShapeDtypeStruct((1, HD), F32),
        ),
        in_specs=[any_, any_, any_, smem, smem, vmem, vmem, any_, vmem, any_],
        out_specs=(vmem,) * 4,
        scratch_shapes=[
            pltpu.VMEM((BAND, ROWS, ROWS), BF16),
            pltpu.VMEM((FAR, TILE, TILE), BF16),
            pltpu.VMEM((HD, ROWS), BF16),
            pltpu.VMEM((NB,) + block, BF16),
            pltpu.VMEM((NB,) + block, BF16),
            pltpu.VMEM((HALF,) + block, BF16),
            pltpu.VMEM((16, 2) + block, BF16),
            pltpu.VMEM((16, 2) + block, BF16),
            pltpu.VMEM((2, 4, NX) + block, BF16),
            pltpu.VMEM((2, 4, NX) + block, BF16),
            pltpu.VMEM((NY,) + block, BF16),
            pltpu.VMEM(block, BF16),
            pltpu.VMEM((NF, HD, ROWS), BF16),
            pltpu.VMEM((NF, HD, ROWS), BF16),
            pltpu.VMEM((NF, HD, ROWS), BF16),
            pltpu.VMEM((NF * HD, NF * HD), F32),
            pltpu.VMEM((NF, HD, ROWS), BF16),
            pltpu.VMEM((NF, 8, 2 * HD), F32),
            pltpu.VMEM((NF, HD, ROWS), F32),
            pltpu.VMEM(block, BF16),
            pltpu.VMEM((FAR + 1, HD, TILE), BF16),
            pltpu.VMEM((BAND,) + block, F32),
            pltpu.VMEM((16, NB), jnp.int32),
            pltpu.SMEM((16, NB), jnp.int32),
            pltpu.VMEM((2, 8, 16, 128), F32),
            pltpu.VMEM((8, 16, 128), F32),
            pltpu.VMEM((8, 16, 128), F32),
            pltpu.VMEM((7, 16, 128), F32),
            pltpu.VMEM((8, 16, 128), F32),
            pltpu.VMEM((8, 16, 128), F32),
            pltpu.VMEM((8, 16, 128), F32),
            dma(6), dma(2), dma(2),
            dma(2, 4, 4), dma(2, 4, 4), dma(2, 4, 4), dma(2, 4, 4),
            dma(2, 8, 2), dma(2, 8, 2), dma(2, 8, 2), dma(2, 8, 2), one, one,
            dma(4, 3), dma(4, 3), dma(16), dma(16),
            dma(16, 2), dma(16, 2), dma(16, 2), dma(16, 2),
            dma(2, 4, 4), dma(2, 4, 4), dma(2, 4, 4), dma(2, 4, 4),
            dma(2), dma(2), dma(7), dma(7), dma(7), dma(7), dma(7), dma(7),
        ],
        compiler_params=pltpu.CompilerParams(
            collective_id=0, has_side_effects=True, vmem_limit_bytes=60 * 2**20
        ),
    )(features, near, far_tiles, source, index, source, index, weight.T, bias[None, :], grad_out)
    return act, gfeat, gw.T, gb[0]


def solution(mesh):
    return jax.shard_map(
        on_device,
        mesh=mesh,
        in_specs=(
            P("feat", "blk"),
            P("blk", None, None),
            P("blk", None, None),
            P("blk", None),
            P("blk", None),
            P(None, "feat"),
            P("feat"),
            P("feat", "blk"),
        ),
        out_specs=(P("feat", "blk"), P("feat", "blk"), P(None, "feat"), P("feat")),
        check_vma=False,
    )
```

```python
import functools

import jax
import jax.numpy as jnp
from jax import lax
from jax.experimental import pallas as pl
from jax.experimental.pallas import tpu as pltpu
from jax.sharding import PartitionSpec as P

NX, NZ, NY, NC = 4, 8, 2, 2
NB = NX * NZ * NY * NC
HALF = NB // NC
GROUP = NX * NY
FAR = 96
BAND = 7
NF = 4
HD = 64
TILE = 128
ROWS = 256
F32 = jnp.float32
BF16 = jnp.bfloat16
NN = (((1,), (0,)), ((), ()))
NT = (((1,), (1,)), ((), ()))
TN = (((0,), (0,)), ((), ()))
STEPS = (4, 3, -3, 2, -2, 1, -1, 0)


def dot(a, b, dims):
    return lax.dot_general(a, b, dims, preferred_element_type=F32)


def send(src, dst, sent, got, **where):
    return pltpu.make_async_remote_copy(
        src_ref=src, dst_ref=dst, send_sem=sent, recv_sem=got,
        device_id=where, device_id_type=pl.DeviceIdType.MESH,
    )


def rem(a, n):
    return lax.rem(a, jnp.int32(n))


def within(n, most):
    return jnp.minimum(jnp.maximum(n, 0), most)


def spot_of(c):
    return (c % 2) * HALF + ((c // 4) % 8) * GROUP + ((c // 2) % 2) * NX + c // 32


def gather_blocks(X, me, share, sy, ry, sR, rR, sL, rL, sXR, rXR, sXL, rXL, sP, rP):
    x, z, y, core, at = me
    east, west = at(rem(x + 1, NX), z, y, core), at(rem(x + NX - 1, NX), z, y, core)
    partner, across = at(x, z, y, 1 - core), at(x, z, 1 - y, core)
    ys = (y, 1 - y)

    def block(k, xx, zz, w):
        return k * HALF + zz * GROUP + ys[w] * NX + xx

    def whole(k, xx, zz, w):
        return X.at[block(k, xx, zz, w)]

    swap = send(whole(core, x, z, 0), whole(core, x, z, 0), sy, ry, blk=across)
    swap.start()

    def swapped():
        send(whole(core, x, z, 1), whole(core, x, z, 1), sy, ry, blk=across).wait_recv()

    def hand(k, zz, w, wait=False):
        ref = X.at[pl.ds(k * HALF + zz * GROUP + ys[w] * NX, NX)]
        copy = send(ref, ref, sP, rP, blk=partner)
        copy.start()

    def ring_parts(k, xx, i, w, wide):
        out = []
        for sign, ss, rr in ((1, sR, rR), (-1, sL, rL)):
            def step(n, zd, hops, half, ss=ss, rr=rr, sign=sign):
                src = whole(k, xx, rem(z + NZ - sign * zd, NZ), w)
                src = src if half is None else src.at[half]
                return send(src, src, ss.at[w, i, n], rr.at[w, i, n], blk=at(x, rem(z + NZ + sign * hops, NZ), y, core))

            half = 0 if sign == 1 else 1
            out.append((
                functools.partial(step, 0, 0, 1, None),
                functools.partial(step, 1, 0, 2, None) if wide else functools.partial(step, 1, 1, 1, None),
                functools.partial(step, 2, 2, 1, None),
                functools.partial(step, 3, 2, 2, half),
            ))
        return out

    def ring_got(k, xx, i, w, n):
        for sign, ss, rr, u in ((1, sR, rR, 0), (-1, sL, rL, 1)):
            ref = whole(k, xx, rem(z + NZ - sign * (n + 1), NZ), w)
            ref = ref if n < 3 else ref.at[u]
            send(ref, ref, ss.at[w, i, n], rr.at[w, i, n], blk=partner).wait_recv()

    def ring_start(k, xx, i, w, wide):
        parts = ring_parts(k, xx, i, w, wide)
        if wide:
            parts[0][1]().start()
            parts[1][1]().start()
        parts[0][0]().start()
        parts[1][0]().start()

    def ring_second(k, xx, i, w):
        ring_got(k, xx, i, w, 0)
        for part in ring_parts(k, xx, i, w, False):
            part[1]().start()

    def ring_third(k, xx, i, w):
        ring_got(k, xx, i, w, 1)
        for part in ring_parts(k, xx, i, w, True):
            part[3]().start()
            part[2]().start()

    def ring_sent(k, xx, i, w, wide):
        for part in ring_parts(k, xx, i, w, wide):
            for copy in part:
                copy().wait_send()

    def x_step(k, zz, j, w, s, what):
        for xx, ss, rr, to, u in ((rem(x + NX - s, NX), sXR, rXR, east, 0), (rem(x + s, NX), sXL, rXL, west, 1)):
            ref = whole(k, xx, zz, w)
            if what == "go" and s > 0:
                got = ref if s < 2 else ref.at[u]
                send(got, got, ss.at[w, j, s - 1], rr.at[w, j, s - 1], blk=to).wait_recv()
            if s < 2:
                out = ref if s < 1 else ref.at[u]
                copy = send(out, out, ss.at[w, j, s], rr.at[w, j, s], blk=to)
                copy.start() if what == "go" else copy.wait_send()

    def places(s):
        if s == 0:
            return [(z, 0)]
        if s == 4:
            return [(rem(z + 4, NZ), 7)]
        return [(rem(z + NZ - s, NZ), 2 * s - 1), (rem(z + s, NZ), 2 * s)]

    def across_x(w):
        ref = whole(1, x, z, w)
        return (
            send(ref, ref, sXR.at[w, 0, 0], rXR.at[w, 0, 0], blk=east),
            send(ref, ref, sXL.at[w, 0, 0], rXL.at[w, 0, 0], blk=west),
            send(ref, ref, sXR.at[w, 0, 1], rXR.at[w, 0, 1], blk=at(rem(x + 2, NX), z, y, core)),
        )

    def from_x(w, i):
        ref = whole(1, rem(x + NX - i, NX), z, w)
        ss, rr, n = ((sXR, rXR, 0), (sXR, rXR, 1), (sXL, rXL, 0))[i - 1]
        send(ref, ref, ss.at[w, 0, n], rr.at[w, 0, n], blk=partner).wait_recv()

    def hop(s, w, n):
        for zz, j in places(s):
            x_step(0, zz, j, w, n, "go")
            if n == 2:
                hand(0, zz, w)

    @pl.when(core == 0)
    def _():
        def got(n, w):
            ring_got(0, x, 0, w, n)
            hop(n + 1, w, 0)

        def third(w):
            ring_third(0, x, 0, w)
            hop(2, w, 0)

        ring_start(0, x, 0, 0, True)
        hop(0, 0, 0)
        third(0)
        got(0, 0)
        swapped()
        ring_start(0, x, 0, 1, True)
        share()
        hop(0, 1, 0)
        hop(0, 0, 1)
        got(2, 0)
        got(3, 0)
        hop(2, 0, 1)
        hop(1, 0, 1)
        hop(0, 0, 2)
        third(1)
        got(0, 1)
        for s, w, n in ((0, 1, 1), (3, 0, 1), (4, 0, 1), (2, 0, 2), (1, 0, 2)):
            hop(s, w, n)
        got(2, 1)
        got(3, 1)
        for s, w, n in (
            (2, 1, 1), (1, 1, 1), (3, 0, 2), (4, 0, 2), (0, 1, 2), (3, 1, 1), (4, 1, 1),
            (2, 1, 2), (1, 1, 2), (3, 1, 2), (4, 1, 2),
        ):
            hop(s, w, n)

    @pl.when(core == 1)
    def _():
        every = (0, 1, 3, 2)

        def xs(i):
            return rem(x + NX - i, NX)

        def spread(w):
            for i in (1, 3, 2):
                from_x(w, i)
                ring_start(1, xs(i), i, w, False)
            hand(1, z, w)

        def second(w, which):
            for i in which:
                ring_second(1, xs(i), i, w)

        def third(w, which):
            for i in which:
                ring_third(1, xs(i), i, w)

        def done(w, n):
            for i in every:
                ring_got(1, xs(i), i, w, n)
            for zz, j in places(n + 1):
                hand(1, zz, w)

        def along(w, n):
            for zz, j in places(n + 1):
                hand(1, zz, w)

        for copy in across_x(0):
            copy.start()
        ring_start(1, x, 0, 0, False)
        spread(0)
        second(0, (0,))
        swapped()
        for copy in across_x(1):
            copy.start()
        ring_start(1, x, 0, 1, False)
        share()
        second(0, (1, 3, 2))
        along(0, 0)
        third(0, (0,))
        spread(1)
        second(1, (0,))
        third(0, (1, 3, 2))
        along(0, 1)
        second(1, (1, 3, 2))
        along(1, 0)
        third(1, (0,))
        done(0, 2)
        done(0, 3)
        third(1, (1, 3, 2))
        along(1, 1)
        done(1, 2)
        done(1, 3)

    theirs = X.at[pl.ds((1 - core) * HALF, HALF)]
    send(theirs, theirs, sP, rP, blk=partner).wait_recv()

    def finish():
        swap.wait_send()
        ours = X.at[pl.ds(core * HALF, HALF)]
        send(ours, ours, sP, rP, blk=partner).wait_send()

        @pl.when(core == 0)
        def _():
            for w in (0, 1):
                ring_sent(0, x, 0, w, True)
                for s in range(5):
                    for zz, j in places(s):
                        x_step(0, zz, j, w, 0, "end")
                        x_step(0, zz, j, w, 1, "end")

        @pl.when(core == 1)
        def _():
            for w in (0, 1):
                for copy in across_x(w):
                    copy.wait_send()
                for i in range(4):
                    ring_sent(1, rem(x + NX - i, NX), i, w, False)

    return finish


def to_feat(S, f, sent, got):
    return [send(S.at[f], S.at[f], sent.at[d - 1], got.at[d - 1], feat=rem(f + d, NF)) for d in (1, 2, 3)]


def from_feat(S, f, sent, got):
    for d in (1, 2, 3):
        ref = S.at[rem(f + NF - d, NF)]
        send(ref, ref, sent.at[d - 1], got.at[d - 1], feat=rem(f + d, NF)).wait_recv()


def add_to(G, at, u, *more):
    if u is None:
        total = G[at].astype(F32)
        for m in more:
            total += m.astype(F32)
        G[at] = total.astype(BF16)
    else:
        total = G[at, u].astype(F32)
        for m in more:
            total += m.astype(F32)
        G[at, u] = total.astype(BF16)


def scatter_blocks(G, H, XE, XW, RR, RL, Fs, Fr, out, me, hooks, sH, rH, sXR, rXR, sXL, rXL, sR, rR, sL, rL, sy, ry):
    x, z, y, core, at = me
    east, west = at(rem(x + 1, NX), z, y, core), at(rem(x + NX - 1, NX), z, y, core)
    partner, across = at(x, z, y, 1 - core), at(x, z, 1 - y, core)
    zs = [rem(z + o + NZ, NZ) for o in STEPS]
    ys = (1 - y, y)
    mine, theirs = core * HALF, (1 - core) * HALF

    def block(xx, j, w):
        return mine + zs[j] * GROUP + ys[w] * NX + xx

    def given(zz, yy, n):
        ref = G.at[pl.ds(theirs + zz * GROUP + yy * NX, NX)]
        return send(ref, H.at[pl.ds(zz * GROUP + yy * NX, NX)], sH.at[n], rH.at[n], blk=partner)

    def taken(j, w):
        base = zs[j] * GROUP + ys[w] * NX
        ref = H.at[pl.ds(base, NX)]
        send(ref, ref, sH.at[j * 2 + w], rH.at[j * 2 + w], blk=partner).wait_recv()
        for n in range(NX):
            add_to(G, mine + base + n, None, H[base + n])

    def ring_copy(xx, i, w, n, way, wide):
        R, ss, rr, sign = (RR, sR, rR, 1) if way == 0 else (RL, sL, rL, -1)
        src = G.at[mine + rem(z + NZ + sign * (n + 1), NZ) * GROUP + ys[w] * NX + xx]
        dst = R.at[w, n, i]
        if n == 3:
            src, dst = src.at[way], dst.at[way]
        hops = 2 if n == 3 or (n == 1 and wide) else 1
        return send(src, dst, ss.at[w, i, n], rr.at[w, i, n], blk=at(x, rem(z + NZ + sign * hops, NZ), y, core))

    def ring_wait(i, w, n, way):
        R, ss, rr = (RR, sR, rR) if way == 0 else (RL, sL, rL)
        ref = R.at[w, n, i, way] if n == 3 else R.at[w, n, i]
        send(ref, ref, ss.at[w, i, n], rr.at[w, i, n], blk=partner).wait_recv()

    def ring(xx, i, j, w, wide):
        if j == 0:
            for way in (0, 1):
                ring_copy(xx, i, w, 3, way, wide).start()
            return
        if j == 7:
            total = G[block(xx, 7, w)].astype(F32)
            for way, R in ((0, RR), (1, RL)):
                for n in (0, 1) if wide else (0,):
                    ring_wait(i, w, n, way)
                    total += R[w, n, i].astype(F32)
            return total
        way, n = (j + 1) % 2, 2 - (j - 1) // 2
        R, base = (RR, RL)[way], block(xx, j, w)
        if n == 1:
            ring_wait(i, w, 3, way)
            ring_wait(i, w, 2, way)
            add_to(G, base, way, R[w, 3, i, way])
            add_to(G, base, None, R[w, 2, i])
        if n == 0 and not wide:
            ring_wait(i, w, 1, way)
            add_to(G, base, None, R[w, 1, i])
        ring_copy(xx, i, w, n, way, wide).start()

    def ring_sent(xx, i, w, wide):
        for n in range(4):
            for way in (0, 1):
                ring_copy(xx, i, w, n, way, wide).wait_send()

    def x_copies(j, w, s):
        far, near_e, near_w = block(rem(x + 2, NX), j, w), block(rem(x + 1, NX), j, w), block(rem(x + NX - 1, NX), j, w)
        n = j * 2 + w
        if s == 0:
            return (send(G.at[far, 0], XE.at[n, 0, 0], sXR.at[n, 0], rXR.at[n, 0], blk=east),
                    send(G.at[far, 1], XW.at[n, 0, 1], sXL.at[n, 0], rXL.at[n, 0], blk=west))
        return (send(G.at[near_e], XE.at[n, 1], sXR.at[n, 1], rXR.at[n, 1], blk=east),
                send(G.at[near_w], XW.at[n, 1], sXL.at[n, 1], rXL.at[n, 1], blk=west))

    def x_step(j, w, s):
        n = j * 2 + w
        if s > 0:
            for copy in x_copies(j, w, s - 1):
                copy.wait_recv()
        if s == 1:
            add_to(G, block(rem(x + 1, NX), j, w), 0, XE[n, 0, 0])
            add_to(G, block(rem(x + NX - 1, NX), j, w), 1, XW[n, 0, 1])
        if s < 2:
            for copy in x_copies(j, w, s):
                copy.start()

    def x_total(j, w):
        n = j * 2 + w
        return G[block(x, j, w)].astype(F32) + XE[n, 1].astype(F32) + XW[n, 1].astype(F32)

    def across_x(w):
        n = 14 + w
        return (
            send(G.at[block(rem(x + 1, NX), 7, w)], XE.at[n, 1], sXR.at[n, 1], rXR.at[n, 1], blk=east),
            send(G.at[block(rem(x + NX - 1, NX), 7, w)], XW.at[n, 1], sXL.at[n, 1], rXL.at[n, 1], blk=west),
            send(G.at[block(rem(x + 2, NX), 7, w)], XE.at[n, 0], sXR.at[n, 0], rXR.at[n, 0], blk=at(rem(x + 2, NX), z, y, core)),
        )

    def from_x(w):
        for copy in across_x(w):
            copy.wait_recv()
        return x_total(7, w) + XE[14 + w, 0].astype(F32)

    order = ((0, 0),) + tuple(o for j in range(1, 8) for o in ((j, 0), (j - 1, 1))) + ((7, 1),)
    last = send(Fs.at[0], Fr, sy, ry, blk=across)

    def deliver(w, total):
        Fs[w] = total.astype(BF16)
        if w == 0:
            last.start()

    def run():
        @pl.when(core == 0)
        def _():
            for n in range(len(order) + 8):
                if n < len(order):
                    taken(*order[n])
                    x_step(*order[n], 0)
                if 0 <= n - 4 < len(order):
                    x_step(*order[n - 4], 1)
                if 0 <= n - 8:
                    j, w = order[n - 8]
                    x_step(j, w, 2)
                    G[block(x, j, w)] = x_total(j, w).astype(BF16)
                    total = ring(x, 0, j, w, True)
                    if j == 7:
                        deliver(w, total)
                if n in hooks:
                    hooks[n]()

        @pl.when(core == 1)
        def _():
            for n, (j, w) in enumerate(order):
                taken(j, w)
                for i in (2, 1, 3, 0):
                    xx = rem(x + i, NX)
                    total = ring(xx, i, j, w, False)
                    if j == 7:
                        G[block(xx, 7, w)] = total.astype(BF16)
                if j == 7:
                    for copy in across_x(w):
                        copy.start()
                if (j, w) == (7, 1):
                    deliver(0, from_x(0))
                    deliver(1, from_x(1))
                if n in hooks:
                    hooks[n]()

        last.wait_recv()
        total = Fs[1].astype(F32) + Fr[...].astype(F32)
        out[:, 0:TILE] = total[0].astype(BF16)
        out[:, TILE:] = total[1].astype(BF16)

    def finish():
        last.wait_send()
        for j in range(8):
            for w in range(2):
                given(zs[j], ys[w], j * 2 + w).wait_send()

        @pl.when(core == 0)
        def _():
            for w in range(2):
                ring_sent(x, 0, w, True)
                for j in range(8):
                    for s in range(2):
                        for copy in x_copies(j, w, s):
                            copy.wait_send()

        @pl.when(core == 1)
        def _():
            for w in range(2):
                for i in range(4):
                    ring_sent(rem(x + i, NX), i, w, False)
                for copy in across_x(w):
                    copy.wait_send()

    return given, run, finish


def kernel(
    feat_hbm, near_hbm, far_hbm, source_ref, index_ref, source_row, index_row, weight_hbm, bias_ref, gout_hbm,
    act_ref, gfeat_ref, gw_ref, gb_ref,
    near, far, feat_in, X, G, H, XE, XW, RR, RL, Fs, Fr, A, GP, WR, WT, GO, BI, BC, ga, parts, band, rows_v, table,
    W0, W1, W2, W3, W5, W7, W8,
    local, sy, ry, sR, rR, sL, rL, sXR, rXR, sXL, rXL, sP, rP,
    sf, rf, sH, rH, tXR, uXR, tXL, uXL, tR, uR, tL, uL, sw, rw, sz, rz, sq, rq, sz2, rz2,
):
    b, f = lax.axis_index("blk"), lax.axis_index("feat")
    core, y, z, x = b % 2, (b // 2) % 2, (b // 4) % 8, b // 32

    def at(xx, zz, yy, cc):
        return ((xx * NZ + zz) * NY + yy) * NC + cc

    me = (x, z, y, core, at)
    partner = at(x, z, y, 1 - core)

    def slab(e):
        return rem(x + e // 2, NX), (y + e % 2) % 2

    def signal(**where):
        pl.semaphore_signal(barrier, 1, device_id=where, device_id_type=pl.DeviceIdType.MESH)

    barrier = pltpu.get_barrier_semaphore()
    signal(blk=partner)
    for e in range(1, 8):
        xx, yy = slab(e)
        signal(blk=at(xx, z, yy, core))
    for d in range(1, NZ):
        signal(blk=at(x, rem(z + d, NZ), y, core))
    for d in (1, 2, 3):
        signal(feat=rem(f + d, NF))

    load_feat = pltpu.make_async_copy(feat_hbm, feat_in, local.at[0])
    load_weight = pltpu.make_async_copy(weight_hbm, WR.at[f], local.at[1])
    load_gout = pltpu.make_async_copy(gout_hbm, GO.at[f], local.at[2])
    load_near = pltpu.make_async_copy(near_hbm, near, local.at[3])
    load_far = pltpu.make_async_copy(far_hbm, far, local.at[4])
    for load in (load_feat, load_weight, load_gout, load_near, load_far):
        load.start()

    BI[f] = jnp.broadcast_to(jnp.concatenate([bias_ref[...], bias_ref[...]], axis=1), (8, 2 * HD))
    load_feat.wait()
    own = core * HALF + z * GROUP + y * NX + x
    X[own, 0] = feat_in[:, 0:TILE]
    X[own, 1] = feat_in[:, TILE:]
    pl.semaphore_wait(barrier, 18)

    load_weight.wait()
    load_gout.wait()

    def share():
        for n, S in ((0, WR), (2, GO), (3, BI)):
            for copy in to_feat(S, f, sf.at[n], rf.at[n]):
                copy.start()

    gathered_all = gather_blocks(X, me, share, sy.at[0], ry.at[0], sR, rR, sL, rL, sXR, rXR, sXL, rXL, sP, rP)

    load_near.wait()
    load_far.wait()
    total = jnp.zeros((HD, ROWS), F32)
    for s in range(BAND):
        spot = spot_of(rem(b + NB + s - 3, NB))
        total += dot(jnp.concatenate([X[spot, 0], X[spot, 1]], axis=1), near[s], NT)

    def far_forward(n, sums):
        low, high = sums
        for r in range(8):
            q = n * 8 + r
            value = dot(X[within(spot_of(source_ref[0, q]), NB - 1), within(index_ref[1, q], 1)], far[q], NT)
            first = index_ref[0, q] == 0
            low += jnp.where(first, value, 0.0)
            high += jnp.where(first, 0.0, value)
        return low, high

    zero = jnp.zeros((HD, TILE), F32)
    low, high = lax.fori_loop(0, FAR // 8, far_forward, (zero, zero))
    A[f] = (total + jnp.concatenate([low, high], axis=1)).astype(BF16)
    for copy in to_feat(A, f, sf.at[1], rf.at[1]):
        copy.start()
    for n, S in ((0, WR), (2, GO), (3, BI)):
        from_feat(S, f, sf.at[n], rf.at[n])
    WT[...] = jnp.transpose(WR[...].reshape(NF * HD, NF * HD).astype(F32))
    for n in range(NF):
        column = jnp.transpose(jnp.broadcast_to(BI[n, 0:1, :], (2 * HD, 2 * HD)))[0:HD]
        BC[n, :, 0:TILE] = column
        BC[n, :, TILE:] = column

    places = jnp.broadcast_to(spot_of(source_row[...]), (NB, FAR))
    keys = jnp.broadcast_to((lax.broadcasted_iota(jnp.int32, (1, FAR), 1) * 2 + index_row[1:2, :]).astype(F32), (NB, FAR))
    match = places == lax.broadcasted_iota(jnp.int32, (NB, FAR), 0)
    one = jnp.min(jnp.where(match, keys, 2.0 * FAR), axis=1, keepdims=True)
    two = jnp.max(jnp.where(match, keys, -1.0), axis=1, keepdims=True)
    two = jnp.where((two == one) | (two < 0.0), 2.0 * FAR, two)
    rows_v[0:8] = jnp.transpose(jnp.broadcast_to(one, (NB, NB)))[0:8].astype(jnp.int32)
    rows_v[8:16] = jnp.transpose(jnp.broadcast_to(two, (NB, NB)))[0:8].astype(jnp.int32)
    load_table = pltpu.make_async_copy(rows_v, table, local.at[5])
    load_table.start()
    from_feat(A, f, sf.at[1], rf.at[1])

    gathered = A[...].reshape(NF * HD, ROWS)
    pre = dot(WR[...].reshape(NF * HD, NF * HD), gathered, NN) + BC[...].reshape(NF * HD, ROWS)
    sig = jax.nn.sigmoid(pre)
    upstream = GO[...].reshape(NF * HD, ROWS).astype(F32)
    every_grad_pre = (upstream * sig * (1.0 + pre * (1.0 - sig))).astype(BF16)
    GP[...] = every_grad_pre.reshape(NF, HD, ROWS)
    grad_pre = GP[f]
    part = dot(grad_pre, gathered, NT)
    ones = dot(jnp.ones((8, ROWS), BF16), grad_pre, NT)
    side = jnp.concatenate([ones, ones], axis=1)
    for k in range(2):
        W0[k, :, 0:8, :] = part[:, k * 128:k * 128 + 128].reshape(8, 8, 128)
        for n in range(8):
            W0[k, n, 8:16, :] = side
    halves = send(W0.at[1 - core], W1, sw.at[0], rw.at[0], blk=partner)
    halves.start()
    own_rows = WT[pl.ds(pl.multiple_of(f * HD, HD), HD), :].astype(BF16)
    grad = dot(own_rows, every_grad_pre, NN).astype(BF16)
    ga[0] = grad[:, 0:TILE]
    ga[1] = grad[:, TILE:]
    pre = dot(WR[f], gathered, NN) + BC[f]
    act_ref[...] = jax.nn.silu(pre).astype(BF16)

    halves.wait_recv()
    W2[...] = W0[core] + W1[...]
    to_z = []
    for d in range(1, NZ):
        zz = rem(z + d, NZ)
        to_z.append(send(W2.at[zz], W3.at[d - 1], sz.at[d - 1], rz.at[d - 1], blk=at(x, zz, y, core)))
        to_z[-1].start()

    def far_backward(n, _):
        for r in range(8):
            q = n * 8 + r
            parts[q] = dot(ga[within(index_ref[0, q], 1)], far[q], NN).astype(BF16)
        return 0

    lax.fori_loop(0, FAR // 8, far_backward, 0)
    parts[FAR] = jnp.zeros((HD, TILE), BF16)
    for s in range(BAND):
        value = dot(grad, near[s], NN)
        band[s, 0] = value[:, 0:TILE]
        band[s, 1] = value[:, TILE:]

    to_slab, again = [], []
    for e in range(1, 8):
        xx, yy = slab(e)
        to_slab.append(send(W5.at[x * NY + y], W5.at[x * NY + y], sq.at[e - 1], rq.at[e - 1], blk=at(xx, z, yy, core)))
    for d in range(1, NZ):
        again.append(send(W7.at[z], W7.at[z], sz2.at[d - 1], rz2.at[d - 1], blk=at(x, rem(z + d, NZ), y, core)))
    final = send(W7, W8, sw.at[1], rw.at[1], blk=partner)

    def sum_z():
        for copy in to_z:
            copy.wait_recv()
        mine = W2[z]
        for d in range(NZ - 1):
            mine += W3[d]
        W5[x * NY + y] = mine
        for copy in to_slab:
            copy.start()

    def sum_slab():
        for e in range(1, 8):
            ref = W5.at[rem(x + NX - e // 2, NX) * NY + (y + e % 2) % 2]
            send(ref, ref, sq.at[e - 1], rq.at[e - 1], blk=partner).wait_recv()
        total = W5[0]
        for n in range(1, 8):
            total += W5[n]
        W7[z] = total
        for copy in again:
            copy.start()

    def spread_z():
        for d in range(1, NZ):
            ref = W7.at[rem(z + NZ - d, NZ)]
            send(ref, ref, sz2.at[d - 1], rz2.at[d - 1], blk=partner).wait_recv()
        final.start()

    sum_z()
    hooks = {6: sum_slab, 14: spread_z}
    given, run, sent = scatter_blocks(
        G, H, XE, XW, RR, RL, Fs, Fr, gfeat_ref, me, hooks,
        sH, rH, tXR, uXR, tXL, uXL, tR, uR, tL, uL, sy.at[1], ry.at[1],
    )

    def place(c):
        one, two = table[0, c], table[8, c]
        va, vb = parts[within(one // 2, FAR)].astype(F32), parts[within(two // 2, FAR)].astype(F32)
        ua, ub = one % 2 == 0, two % 2 == 0
        G[c, 0] = (jnp.where(ua, va, 0.0) + jnp.where(ub, vb, 0.0)).astype(BF16)
        G[c, 1] = (jnp.where(ua, 0.0, va) + jnp.where(ub, 0.0, vb)).astype(BF16)

    def group(j, w):
        return rem(z + 4 + j // 2 + (j % 2) * (NZ - j), NZ), (1 - y, y)[w]

    def fill(j, w):
        zz, yy = group(j, w)
        for k in (1 - core, core):
            for r in range(NX):
                place(k * HALF + zz * GROUP + yy * NX + r)

    def give(j, w):
        zz, yy = group(j, w)
        given(zz, yy, j * 2 + w).start()

    def fill_and_give(j, _):
        for w in (0, 1):
            fill(j, w)
            give(j, w)
        return 0

    def fill_near(j, _):
        fill(j, 0)
        fill(j, 1)
        return 0

    load_table.wait()
    lax.fori_loop(0, 5, fill_and_give, 0)
    lax.fori_loop(5, 8, fill_near, 0)
    for s in range(BAND):
        spot = spot_of(rem(b + NB + s - 3, NB))
        G[spot] = (G[spot].astype(F32) + band[s]).astype(BF16)
    for j in (5, 6, 7):
        give(j, 0)
        give(j, 1)

    run()
    final.wait_recv()
    for k in range(2):
        value = jnp.where(core == k, W7[...], W8[...])
        gw_ref[:, k * 128:k * 128 + 128] = value[:, 0:8, :].reshape(HD, 128)
    gb_ref[...] = jnp.where(core == 0, W7[0, 8:9, :], W8[0, 8:9, :])[:, 0:HD]

    gathered_all()
    sent()
    halves.wait_send()
    for n, S in enumerate((WR, A, GO, BI)):
        for copy in to_feat(S, f, sf.at[n], rf.at[n]):
            copy.wait_send()
    for copy in to_z + to_slab + again + [final]:
        copy.wait_send()


def on_device(features, near_tiles, far_tiles, far_source, far_index, weight, bias, grad_out):
    near = jnp.transpose(near_tiles, (1, 0, 2))
    source, index = far_source.T, far_index.T
    vmem, smem, any_ = (pl.BlockSpec(memory_space=s) for s in (pltpu.VMEM, pltpu.SMEM, pl.ANY))
    dma = lambda *shape: pltpu.SemaphoreType.DMA(shape)
    one = pltpu.SemaphoreType.DMA
    block = (2, HD, TILE)
    act, gfeat, gw, gb = pl.pallas_call(
        kernel,
        out_shape=(
            jax.ShapeDtypeStruct((HD, ROWS), BF16),
            jax.ShapeDtypeStruct((HD, ROWS), BF16),
            jax.ShapeDtypeStruct((HD, NF * HD), F32),
            jax.ShapeDtypeStruct((1, HD), F32),
        ),
        in_specs=[any_, any_, any_, smem, smem, vmem, vmem, any_, vmem, any_],
        out_specs=(vmem,) * 4,
        scratch_shapes=[
            pltpu.VMEM((BAND, ROWS, ROWS), BF16),
            pltpu.VMEM((FAR, TILE, TILE), BF16),
            pltpu.VMEM((HD, ROWS), BF16),
            pltpu.VMEM((NB,) + block, BF16),
            pltpu.VMEM((NB,) + block, BF16),
            pltpu.VMEM((HALF,) + block, BF16),
            pltpu.VMEM((16, 2) + block, BF16),
            pltpu.VMEM((16, 2) + block, BF16),
            pltpu.VMEM((2, 4, NX) + block, BF16),
            pltpu.VMEM((2, 4, NX) + block, BF16),
            pltpu.VMEM((NY,) + block, BF16),
            pltpu.VMEM(block, BF16),
            pltpu.VMEM((NF, HD, ROWS), BF16),
            pltpu.VMEM((NF, HD, ROWS), BF16),
            pltpu.VMEM((NF, HD, ROWS), BF16),
            pltpu.VMEM((NF * HD, NF * HD), F32),
            pltpu.VMEM((NF, HD, ROWS), BF16),
            pltpu.VMEM((NF, 8, 2 * HD), F32),
            pltpu.VMEM((NF, HD, ROWS), F32),
            pltpu.VMEM(block, BF16),
            pltpu.VMEM((FAR + 1, HD, TILE), BF16),
            pltpu.VMEM((BAND,) + block, F32),
            pltpu.VMEM((16, NB), jnp.int32),
            pltpu.SMEM((16, NB), jnp.int32),
            pltpu.VMEM((2, 8, 16, 128), F32),
            pltpu.VMEM((8, 16, 128), F32),
            pltpu.VMEM((8, 16, 128), F32),
            pltpu.VMEM((7, 16, 128), F32),
            pltpu.VMEM((8, 16, 128), F32),
            pltpu.VMEM((8, 16, 128), F32),
            pltpu.VMEM((8, 16, 128), F32),
            dma(6), dma(2), dma(2),
            dma(2, 4, 4), dma(2, 4, 4), dma(2, 4, 4), dma(2, 4, 4),
            dma(2, 8, 2), dma(2, 8, 2), dma(2, 8, 2), dma(2, 8, 2), one, one,
            dma(4, 3), dma(4, 3), dma(16), dma(16),
            dma(16, 2), dma(16, 2), dma(16, 2), dma(16, 2),
            dma(2, 4, 4), dma(2, 4, 4), dma(2, 4, 4), dma(2, 4, 4),
            dma(2), dma(2), dma(7), dma(7), dma(7), dma(7), dma(7), dma(7),
        ],
        compiler_params=pltpu.CompilerParams(
            collective_id=0, has_side_effects=True, vmem_limit_bytes=60 * 2**20
        ),
    )(features, near, far_tiles, source, index, source, index, weight.T, bias[None, :], grad_out)
    return act, gfeat, gw.T, gb[0]


def solution(mesh):
    return jax.shard_map(
        on_device,
        mesh=mesh,
        in_specs=(
            P("feat", "blk"),
            P("blk", None, None),
            P("blk", None, None),
            P("blk", None),
            P("blk", None),
            P(None, "feat"),
            P("feat"),
            P("feat", "blk"),
        ),
        out_specs=(P("feat", "blk"), P("feat", "blk"), P(None, "feat"), P("feat")),
        check_vma=False,
    )
```
